512 devices in a mesh: ctx: 32 (over y, x, core), chan: 16 (over z).
Axes of the slice: x: 4, y: 4, z: 16, core: 2. Of those that a mesh axis runs over, the one named last changes fastest.
Arguments:
- value_branch: bfloat16 [192, 262144], P(None, ('ctx', 'chan')), may hold values from -6 to 6
- key_branch: bfloat16 [192, 262144], P(None, ('ctx', 'chan')), may hold values from -6 to 6
- gate_branch: bfloat16 [192, 262144], P(None, ('ctx', 'chan')), may hold values from -6 to 6
- skip_gain: float32 [192], replicated, may hold values from -4 to 4
- spectra: float32 [2, 192, 32, 8192], P(None, 'chan', 'ctx'), may hold values from -6 to 6
Outputs:
- gated_output: bfloat16 [192, 262144], P(None, ('ctx', 'chan'))
The draws below stay inside these ranges and needn't reach their ends.
All inputs are finite; a program needn't handle non-finite values.
Results may differ from the reference program's by a relative error of at most 0.0054.
Values may be sent and summed in bfloat16 or wider, within the bound.
No kernel may reach another device: no remote copies, remote signals or barrier semaphores. Data moves between devices by JAX's collectives and lax.ppermute only.
A program may use at most 64 MiB of HBM per device.

```python
import jax
import jax.numpy as jnp
import numpy as np
from jax import lax

CHANNELS = 192
SEQ_DEV = 8192
LENGTH = 262144
N_CTX = 32


def steps_of(rng, shape, cuts, least, high):
    level, own = 1.0, jax.random.fold_in(rng, 6)
    for dim, blocks in cuts:
        steps = jnp.exp(jax.random.uniform(jax.random.fold_in(own, dim), (blocks,), jnp.float32, least / len(cuts), high / len(cuts)))
        level = level * jnp.repeat(steps, shape[dim] // blocks).reshape([-1 if axis == dim else 1 for axis in range(len(shape))])
    return level


def scatter_about(key, dims, width, most, cuts=(), held_as=jnp.bfloat16):
    entries = width * jax.random.normal(key, dims, jnp.float32)
    if cuts:
        entries = entries * steps_of(key, dims, cuts, -0.22, 0.18)
    return jnp.clip(entries, -most, most).astype(held_as)


def setup_inputs(seed: int = 0) -> dict:
    keys = jax.random.split(jax.random.key(seed), 6)
    value_branch = scatter_about(keys[0], (CHANNELS, LENGTH), 1.0, 6.0, ((1, 512),))
    key_branch = scatter_about(keys[1], (CHANNELS, LENGTH), 1.0, 6.0, ((1, 512),))
    gate_branch = scatter_about(keys[2], (CHANNELS, LENGTH), 1.0, 6.0, ((1, 512),))
    skip_gain = scatter_about(keys[3], (CHANNELS,), 1.0, 4.0, (), jnp.float32)
    spectra = scatter_about(keys[4], (2, CHANNELS, N_CTX, SEQ_DEV), 1.0, 6.0, ((1, 16), (2, 32)), jnp.float32)
    return dict(value_branch=value_branch, key_branch=key_branch, gate_branch=gate_branch, skip_gain=skip_gain, spectra=spectra)


def reversed_bits(numbers, bit_count):
    result = numbers * 0
    for bit_number in range(bit_count):
        result = result + ((numbers >> bit_number) & 1) * (1 << (bit_count - 1 - bit_number))
    return result


def reference(value_branch, key_branch, gate_branch, skip_gain, spectra):
    carried = (key_branch.astype(jnp.float32) * value_branch.astype(jnp.float32)).astype(jnp.bfloat16)
    bit_count = N_CTX.bit_length() - 1
    reversed_order = reversed_bits(np.arange(N_CTX), bit_count)

    def convolve(packed):
        signal, filter_real, filter_imag = packed
        natural_real = jnp.swapaxes(filter_real[reversed_order, :], 0, 1).reshape(-1)
        natural_imag = jnp.swapaxes(filter_imag[reversed_order, :], 0, 1).reshape(-1)
        transformed = jnp.fft.fft(signal.astype(jnp.float32))
        shaped = transformed * (natural_real + 1j * natural_imag)
        return jnp.real(jnp.fft.ifft(shaped)).astype(jnp.float32)

    convolved = lax.map(convolve, (carried, spectra[0], spectra[1])).astype(jnp.bfloat16)
    result = gate_branch.astype(jnp.float32) * (convolved.astype(jnp.float32) + skip_gain[:, None] * carried.astype(jnp.float32))
    return result.astype(jnp.bfloat16)
```

```python
import math

import jax
import jax.numpy as jnp
import ml_dtypes
import numpy as np
from jax import lax
from jax.experimental import pallas as pl
from jax.experimental.pallas import tpu as pltpu
from jax.sharding import PartitionSpec as P

N_CTX = 32
N_CHAN = 16
CHANNELS = 192
GROUP = CHANNELS // N_CHAN
TOKENS = 512
SEQ = 8192
LENGTH = SEQ * N_CTX
LANES = 128
F32 = jnp.float32
BF16 = jnp.bfloat16
VMEM_LIMIT = 32 * 1024 * 1024


def rev5(number):
    return int(f"{number:05b}"[::-1], 2)


def c_add(a, b):
    im = a[1] if b[1] is None else (b[1] if a[1] is None else a[1] + b[1])
    return (a[0] + b[0], im)


def c_sub(a, b):
    if b[1] is None:
        im = a[1]
    else:
        im = -b[1] if a[1] is None else a[1] - b[1]
    return (a[0] - b[0], im)


def c_root(a, turn, sign):
    if turn == 0:
        return a
    if turn == 0.25:
        if a[1] is None:
            return (jnp.zeros_like(a[0]), sign * a[0])
        return (-sign * a[1], sign * a[0])
    cosine = math.cos(2 * math.pi * turn)
    sine = sign * math.sin(2 * math.pi * turn)
    if a[1] is None:
        return (a[0] * cosine, a[0] * sine)
    if turn in (0.125, 0.375):
        root = math.sqrt(0.5)
        s_c = 1.0 if cosine > 0 else -1.0
        s_s = 1.0 if sine > 0 else -1.0
        re = a[0] - a[1] if s_c * s_s > 0 else a[0] + a[1]
        im = a[0] + a[1] if s_c * s_s > 0 else a[1] - a[0]
        return (re * (s_c * root), im * (s_c * root))
    return (a[0] * cosine - a[1] * sine, a[0] * sine + a[1] * cosine)


def c_mul(a, re, im):
    return (a[0] * re - a[1] * im, a[0] * im + a[1] * re)


def fft_list(terms, sign):
    size = len(terms)
    if size == 1:
        return terms
    half = size // 2
    even = fft_list(terms[0::2], sign)
    odd = fft_list(terms[1::2], sign)
    odd = [c_root(term, index / size, sign) for index, term in enumerate(odd)]
    return [c_add(e, o) for e, o in zip(even, odd)] + [c_sub(e, o) for e, o in zip(even, odd)]


def halves_sum(x, sign_rows):
    return x * sign_rows + pltpu.roll(x, 4, 0)


def pack_kernel(key_ref, value_ref, out_ref, wide):
    low = lax.broadcasted_iota(jnp.int32, (8, LANES), 0) < 4
    for block in range(CHANNELS // 16):
        rows = slice(16 * block, 16 * block + 16)
        carried = (key_ref[rows, :].astype(F32) * value_ref[rows, :].astype(F32)).astype(BF16).astype(F32)
        for part in range(2):
            for upper in range(2):
                a = carried[8 * part : 8 * part + 8, 256 * upper : 256 * upper + 128]
                b = carried[8 * part : 8 * part + 8, 256 * upper + 128 : 256 * upper + 256]
                first = jnp.where(low, a, pltpu.roll(b, 4, 0))
                second = jnp.where(low, pltpu.roll(a, 4, 0), b)
                for offset, piece in enumerate((first, second)):
                    quad = 4 * block + 2 * part + offset
                    start = 24 * upper + 8 * (quad % 3)
                    wide[quad // 3, start : start + 8, :] = piece
    for target in range(N_CHAN):
        out_ref[target] = wide[target].astype(BF16)


def gate_kernel(conv_ref, key_ref, value_ref, gate_ref, skip_ref, out_ref, wide, flat):
    low = lax.broadcasted_iota(jnp.int32, (8, LANES), 0) < 4
    for source in range(N_CHAN):
        wide[source] = conv_ref[source].astype(F32)
    for block in range(CHANNELS // 8):
        for upper in range(2):
            pieces = []
            for offset in range(2):
                quad = 2 * block + offset
                start = 24 * upper + 8 * (quad % 3)
                pieces.append(wide[quad // 3, start : start + 8, :])
            first, second = pieces
            flat[8 * block : 8 * block + 8, 256 * upper : 256 * upper + 128] = jnp.where(
                low, first, pltpu.roll(second, 4, 0)
            )
            flat[8 * block : 8 * block + 8, 256 * upper + 128 : 256 * upper + 256] = jnp.where(
                low, pltpu.roll(first, 4, 0), second
            )
    for block in range(CHANNELS // 16):
        rows = slice(16 * block, 16 * block + 16)
        carried = (key_ref[rows, :].astype(F32) * value_ref[rows, :].astype(F32)).astype(BF16).astype(F32)
        total = flat[rows, :] + skip_ref[rows, :] * carried
        out_ref[rows, :] = (gate_ref[rows, :].astype(F32) * total).astype(BF16)


def blocks_forward_kernel(in_ref, out_ref, wide, result):
    for pair in range(N_CTX // 2):
        wide[pair] = in_ref[pair].astype(F32)
    for group in range(3):
        rows = [slice(24 * half + 8 * group, 24 * half + 8 * group + 8) for half in range(2)]
        terms = [(wide[p // 2, rows[p % 2], :], None) for p in range(N_CTX)]
        sums = fft_list(terms, -1)
        for residue in range(N_CTX):
            if residue <= N_CTX // 2:
                re, im = sums[residue]
                if im is None:
                    im = jnp.zeros_like(re)
            else:
                re, im = sums[N_CTX - residue]
                im = -im
            target = rev5(residue)
            result[target, 8 * group : 8 * group + 8, :] = re
            result[target, 24 + 8 * group : 32 + 8 * group, :] = im
    for target in range(N_CTX):
        out_ref[target] = result[target].astype(BF16)


def blocks_inverse_kernel(in_ref, out_ref, wide, result):
    for source in range(N_CTX):
        wide[source] = in_ref[source].astype(F32)
    for group in range(3):
        terms = []
        for residue in range(N_CTX):
            source = rev5(residue)
            terms.append(
                (
                    wide[source, 8 * group : 8 * group + 8, :],
                    wide[source, 24 + 8 * group : 32 + 8 * group, :],
                )
            )
        sums = fft_list(terms, 1)
        for p in range(N_CTX):
            start = 24 * (p % 2) + 8 * group
            result[p // 2, start : start + 8, :] = sums[p][0]
    for pair in range(N_CTX // 2):
        out_ref[pair] = result[pair].astype(BF16)


def split_dot(x, high, low):
    x_high = x.astype(BF16)
    x_low = (x - x_high.astype(F32)).astype(BF16)
    total = jnp.dot(x_high, high, preferred_element_type=F32)
    total += jnp.dot(x_low, high, preferred_element_type=F32)
    total += jnp.dot(x_high, low, preferred_element_type=F32)
    return total


def filter_kernel(in_ref, spectra_ref, near_ref, far_ref, matrix_ref, out_ref, wide, rows_ref):
    row = lax.broadcasted_iota(jnp.int32, (8, LANES), 0)
    low = row < 4
    sign_rows = jnp.where(low, 1.0, -1.0).astype(F32)
    for q in range(N_CTX):
        wide[q] = in_ref[q].astype(F32)

    def pair_phase(kq, sign):
        turn = 2 * math.pi * kq / 64
        return (
            jnp.where(low, 1.0, math.cos(turn)).astype(F32),
            jnp.where(low, 0.0, sign * math.sin(turn)).astype(F32),
        )

    for group in range(3):
        terms = []
        for q in range(N_CTX):
            term = (
                wide[q, 8 * group : 8 * group + 8, :],
                wide[q, 24 + 8 * group : 32 + 8 * group, :],
            )
            terms.append(c_mul(term, near_ref[0, q], near_ref[1, q]))
        sums = fft_list(terms, -1)
        for kq in range(N_CTX):
            term = sums[kq]
            if kq:
                term = c_mul(term, *pair_phase(kq, -1))
            term = (halves_sum(term[0], sign_rows), halves_sum(term[1], sign_rows))
            term = c_mul(term, far_ref[0, kq], far_ref[1, kq])
            start = 24 * kq + 8 * group
            rows_ref[start : start + 8, 0:LANES] = term[0]
            rows_ref[start : start + 8, LANES : 2 * LANES] = term[1]
    chunk = 192
    for index in range(768 // chunk):
        rows = slice(chunk * index, chunk * index + chunk)
        spectrum = split_dot(rows_ref[rows, :], matrix_ref[0], matrix_ref[1])
        re, im = spectrum[:, :LANES], spectrum[:, LANES:]
        response_re, response_im = spectra_ref[0, rows, :], spectra_ref[1, rows, :]
        shaped = jnp.concatenate(
            [re * response_re - im * response_im, re * response_im + im * response_re], axis=1
        )
        rows_ref[rows, :] = split_dot(shaped, matrix_ref[2], matrix_ref[3])
    for group in range(3):
        terms = []
        for kq in range(N_CTX):
            start = 24 * kq + 8 * group
            term = (rows_ref[start : start + 8, 0:LANES], rows_ref[start : start + 8, LANES : 2 * LANES])
            term = c_mul(term, far_ref[0, kq], -far_ref[1, kq])
            term = (halves_sum(term[0], sign_rows), halves_sum(term[1], sign_rows))
            if kq:
                term = c_mul(term, *pair_phase(kq, 1))
            terms.append(term)
        sums = fft_list(terms, 1)
        for q in range(N_CTX):
            term = c_mul(sums[q], near_ref[0, q], -near_ref[1, q])
            wide[q, 8 * group : 8 * group + 8, :] = term[0]
            wide[q, 24 + 8 * group : 32 + 8 * group, :] = term[1]
    for q in range(N_CTX):
        out_ref[q] = wide[q].astype(BF16)


def far_table():
    kq = np.arange(32)[:, None, None]
    h = (np.arange(8) // 4)[None, :, None]
    lane = np.arange(LANES)[None, None, :]
    angle = -2 * np.pi * ((lane * (kq + 32 * h)) % SEQ) / SEQ
    return np.stack([np.cos(angle), np.sin(angle)]).astype(np.float32)


def lane_matrices():
    counter = np.arange(LANES)
    angle = 2 * np.pi * ((counter[:, None] * counter[None, :]) % LANES) / LANES
    cosine, sine = np.cos(angle), np.sin(angle)
    forward = np.block([[cosine, -sine], [sine, cosine]])
    inverse = np.block([[cosine, sine], [-sine, cosine]]) / LENGTH
    parts = []
    for matrix in (forward, inverse):
        high = matrix.astype(ml_dtypes.bfloat16)
        parts += [high, (matrix - high.astype(np.float64)).astype(ml_dtypes.bfloat16)]
    return np.stack(parts)


def near_table(residue):
    q = lax.broadcasted_iota(jnp.int32, (N_CTX, 8, LANES), 0)
    h = lax.broadcasted_iota(jnp.int32, (N_CTX, 8, LANES), 1) // 4
    lane = lax.broadcasted_iota(jnp.int32, (N_CTX, 8, LANES), 2)
    angle = (-2 * math.pi / LENGTH) * ((256 * q + 128 * h + lane) * residue).astype(F32)
    return jnp.stack([jnp.cos(angle), jnp.sin(angle)])


def call(kernel, out_shape, scratch, *operands):
    return pl.pallas_call(
        kernel,
        out_shape=jax.ShapeDtypeStruct(*out_shape),
        in_specs=[pl.BlockSpec(memory_space=pltpu.VMEM)] * len(operands),
        out_specs=pl.BlockSpec(memory_space=pltpu.VMEM),
        scratch_shapes=[pltpu.VMEM(shape, F32) for shape in scratch],
        compiler_params=pltpu.CompilerParams(vmem_limit_bytes=VMEM_LIMIT),
    )(*operands)


def exchange(x, axis):
    return lax.all_to_all(x, axis, split_axis=0, concat_axis=0, tiled=True)


def body(value_branch, key_branch, gate_branch, skip_gain, spectra):
    device = lax.axis_index("ctx")
    residue = sum(((device >> bit) & 1) << (4 - bit) for bit in range(5))
    near = near_table(residue)
    far = jnp.asarray(far_table())
    matrices = jnp.asarray(lane_matrices())
    response = spectra.reshape(2, 3, 4, LANES, 2, 32).transpose(0, 5, 1, 4, 2, 3).reshape(2, 768, LANES)

    packed = call(pack_kernel, ((N_CHAN, 48, LANES), BF16), [(N_CHAN, 48, LANES)], key_branch, value_branch)
    series = exchange(packed, "chan").reshape(N_CTX, 24, LANES)
    blocks = exchange(series, "ctx").reshape(N_CTX // 2, 48, LANES)
    rows = call(
        blocks_forward_kernel,
        ((N_CTX, 48, LANES), BF16),
        [(N_CTX // 2, 48, LANES), (N_CTX, 48, LANES)],
        blocks,
    )
    received = exchange(rows, "ctx")
    returned = call(
        filter_kernel,
        ((N_CTX, 48, LANES), BF16),
        [(N_CTX, 48, LANES), (768, 2 * LANES)],
        received,
        response,
        near,
        far,
        matrices,
    )
    parts = exchange(returned, "ctx")
    local = call(
        blocks_inverse_kernel,
        ((N_CTX // 2, 48, LANES), BF16),
        [(N_CTX, 48, LANES), (N_CTX // 2, 48, LANES)],
        parts,
    )
    convolved = exchange(local.reshape(N_CTX, 24, LANES), "ctx").reshape(N_CHAN, 48, LANES)
    tokens = exchange(convolved, "chan")
    return call(
        gate_kernel,
        ((CHANNELS, TOKENS), BF16),
        [(N_CHAN, 48, LANES), (CHANNELS, TOKENS)],
        tokens,
        key_branch,
        value_branch,
        gate_branch,
        skip_gain[:, None],
    )


def solution(mesh):
    in_specs = (
        P(None, ("ctx", "chan")),
        P(None, ("ctx", "chan")),
        P(None, ("ctx", "chan")),
        P(),
        P(None, "chan", "ctx", None),
    )
    out_specs = P(None, ("ctx", "chan"))
    return jax.shard_map(body, mesh=mesh, in_specs=in_specs, out_specs=out_specs, check_vma=False)
```

```python
import math

import jax
import jax.numpy as jnp
import ml_dtypes
import numpy as np
from jax import lax
from jax.experimental import pallas as pl
from jax.experimental.pallas import tpu as pltpu
from jax.sharding import PartitionSpec as P

N_CTX = 32
N_CHAN = 16
CHANNELS = 192
GROUP = CHANNELS // N_CHAN
TOKENS = 512
SEQ = 8192
LENGTH = SEQ * N_CTX
LANES = 128
HALF = 16
ROWS = SEQ // LANES
F32 = jnp.float32
BF16 = jnp.bfloat16
VMEM_LIMIT = 32 * 1024 * 1024


def rev4(number):
    return int(f"{number:04b}"[::-1], 2)


def c_root(a, turn, sign):
    if turn == 0:
        return a
    if turn == 0.25:
        return (-a[1], a[0]) if sign > 0 else (a[1], -a[0])
    cosine = math.cos(2 * math.pi * turn)
    sine = sign * math.sin(2 * math.pi * turn)
    return (a[0] * cosine - a[1] * sine, a[0] * sine + a[1] * cosine)


def c_mul(a, re, im):
    return (a[0] * re - a[1] * im, a[0] * im + a[1] * re)


def fft_list(terms, sign):
    size = len(terms)
    if size == 1:
        return terms
    even = fft_list(terms[0::2], sign)
    odd = fft_list(terms[1::2], sign)
    odd = [c_root(term, index / size, sign) for index, term in enumerate(odd)]
    return [(e[0] + o[0], e[1] + o[1]) for e, o in zip(even, odd)] + [
        (e[0] - o[0], e[1] - o[1]) for e, o in zip(even, odd)
    ]


def product_kernel(key_ref, value_ref, out_ref, flat, wide):
    for block in range(CHANNELS // 16):
        rows = slice(16 * block, 16 * block + 16)
        product = key_ref[rows, :].astype(F32) * value_ref[rows, :].astype(F32)
        flat[rows, :] = product
    for target in range(N_CHAN):
        for quarter in range(4):
            wide[target, GROUP * quarter : GROUP * quarter + GROUP, :] = flat[
                GROUP * target : GROUP * target + GROUP, LANES * quarter : LANES * quarter + LANES
            ]
    for target in range(N_CHAN):
        out_ref[target] = wide[target].astype(BF16)


def fan_out_kernel(in_ref, out_ref, wide):
    for source in range(N_CHAN):
        wide[48 * source : 48 * source + 48, :] = in_ref[source].astype(F32)
    for channel in range(GROUP):
        series = wide[pl.ds(channel, ROWS, stride=GROUP), :].astype(BF16)
        out_ref[channel] = series
        out_ref[HALF + channel] = series
    for channel in range(GROUP, HALF):
        empty = jnp.zeros((ROWS, LANES), BF16)
        out_ref[channel] = empty
        out_ref[HALF + channel] = empty


def join_kernel(in_ref, out_ref, wide):
    for channel in range(GROUP):
        total = in_ref[channel].astype(F32) + in_ref[HALF + channel].astype(F32)
        wide[pl.ds(channel, ROWS, stride=GROUP), :] = total
    for target in range(N_CHAN):
        out_ref[target] = wide[48 * target : 48 * target + 48, :].astype(BF16)


def gate_kernel(conv_ref, key_ref, value_ref, gate_ref, skip_ref, out_ref, wide, flat):
    for source in range(N_CHAN):
        wide[source] = conv_ref[source].astype(F32)
    for source in range(N_CHAN):
        for quarter in range(4):
            flat[GROUP * source : GROUP * source + GROUP, LANES * quarter : LANES * quarter + LANES] = wide[
                source, GROUP * quarter : GROUP * quarter + GROUP, :
            ]
    for block in range(CHANNELS // 16):
        rows = slice(16 * block, 16 * block + 16)
        carried = (key_ref[rows, :].astype(F32) * value_ref[rows, :].astype(F32)).astype(BF16).astype(F32)
        total = flat[rows, :] + skip_ref[rows, :] * carried
        out_ref[rows, :] = (gate_ref[rows, :].astype(F32) * total).astype(BF16)


def spectra_kernel(place_ref, in_ref, out_ref):
    place = place_ref[0]
    for channel in range(GROUP):
        slot = place ^ channel
        parts = []
        for part in range(2):
            turned = in_ref[part, channel].T
            parts.append(jnp.concatenate([turned[:64, :], turned[64:, :]], axis=1))
        out_ref[slot] = jnp.concatenate(parts, axis=0).astype(BF16)
    for channel in range(GROUP, HALF):
        out_ref[place ^ channel] = jnp.zeros((2 * ROWS, LANES), BF16)


def split(x):
    high = x.astype(BF16)
    return high, (x - high.astype(F32)).astype(BF16)


def dot(a, b):
    return jnp.dot(a, b, preferred_element_type=F32)


def filter_kernel(
    place_ref, in_ref, spectra_ref, parity_ref, block_ref, lane_ref, row_matrix_ref, lane_matrix_ref, out_ref, real, pair
):
    place = place_ref[0]
    odd = place_ref[1]
    sign = jnp.where(odd == 0, 1.0, -1.0).astype(F32)

    def entry_phase(index, rows):
        cosine = jnp.where(odd == 0, 1.0, math.cos(math.pi * index / HALF)).astype(F32)
        sine = jnp.where(odd == 0, 0.0, -math.sin(math.pi * index / HALF)).astype(F32)
        re, im = parity_ref[0, rows, :], parity_ref[1, rows, :]
        re = jnp.where(odd == 0, 1.0, re)
        im = jnp.where(odd == 0, 0.0, im)
        return (re * cosine - im * sine, re * sine + im * cosine)

    for index in range(HALF):
        real[index] = in_ref[index].astype(F32) + sign * in_ref[HALF + index].astype(F32)
    for group in range(ROWS // 8):
        rows = slice(8 * group, 8 * group + 8)
        terms = []
        for index in range(HALF):
            phase = entry_phase(index, rows)
            term = real[index, rows, :]
            terms.append((term * phase[0], term * phase[1]))
        for kp, term in enumerate(fft_list(terms, -1)):
            if kp:
                term = c_mul(term, block_ref[0, kp, rows, :], block_ref[1, kp, rows, :])
            pair[kp, 8 * group : 8 * group + 8, :] = term[0]
            pair[kp, ROWS + 8 * group : ROWS + 8 * group + 8, :] = term[1]
    lane_re, lane_im = lane_ref[0], lane_ref[1]
    for kp in range(HALF):
        high, low = split(pair[kp])
        mixed = dot(row_matrix_ref[0], jnp.concatenate([high, low, high], axis=0))
        term = c_mul((mixed[:ROWS], mixed[ROWS:]), lane_re, lane_im)
        high, low = split(jnp.concatenate(term, axis=1))
        spectrum = dot(high, lane_matrix_ref[0]) + (dot(low, lane_matrix_ref[0]) + dot(high, lane_matrix_ref[1]))
        response = spectra_ref[place ^ rev4(kp)].astype(F32)
        term = c_mul((spectrum[:, :LANES], spectrum[:, LANES:]), response[:ROWS], response[ROWS:])
        high, low = split(jnp.concatenate(term, axis=1))
        mixed = dot(high, lane_matrix_ref[2]) + (dot(low, lane_matrix_ref[2]) + dot(high, lane_matrix_ref[3]))
        term = c_mul((mixed[:, :LANES], mixed[:, LANES:]), lane_re, -lane_im)
        high, low = split(jnp.concatenate(term, axis=0))
        pair[kp] = dot(row_matrix_ref[1], jnp.concatenate([high, low, high], axis=0))
    for group in range(ROWS // 8):
        rows = slice(8 * group, 8 * group + 8)
        terms = []
        for kp in range(HALF):
            term = (pair[kp, 8 * group : 8 * group + 8, :], pair[kp, ROWS + 8 * group : ROWS + 8 * group + 8, :])
            if kp:
                term = c_mul(term, block_ref[0, kp, rows, :], -block_ref[1, kp, rows, :])
            terms.append(term)
        for index, term in enumerate(fft_list(terms, 1)):
            phase = entry_phase(index, rows)
            real[index, rows, :] = term[0] * phase[0] + term[1] * phase[1]
    for index in range(HALF):
        total = real[index]
        out_ref[index] = total.astype(BF16)
        out_ref[HALF + index] = (sign * total).astype(BF16)


def phases(numerator, denominator):
    angle = -2 * np.pi * (numerator % denominator) / denominator
    return np.cos(angle), np.sin(angle)


def tables():
    row, lane = np.arange(ROWS), np.arange(LANES)
    offset = (LANES * row[:, None] + lane[None, :])[None]
    kp = np.arange(HALF)[:, None, None]
    parity = np.stack(phases(offset[0], LENGTH)).astype(np.float32)
    block = np.stack(phases(2 * kp * offset, LENGTH)).astype(np.float32)
    lane_phase = np.stack(phases(row[:, None] * lane[None, :], SEQ)).astype(np.float32)

    def parts(matrix):
        high = matrix.astype(ml_dtypes.bfloat16)
        return high, (matrix - high.astype(np.float64)).astype(ml_dtypes.bfloat16)

    cosine, sine = phases(row[:, None] * row[None, :], ROWS)
    row_matrices = []
    for flip in (1, -1):
        high, low = parts(np.block([[cosine, -flip * sine], [flip * sine, cosine]]))
        row_matrices.append(np.concatenate([high, high, low], axis=1))
    order = np.concatenate([np.arange(0, LANES, 2), np.arange(1, LANES, 2)])
    cosine, sine = phases(lane[:, None] * order[None, :], LANES)
    forward = np.block([[cosine, sine], [-sine, cosine]])
    inverse = np.block([[cosine.T, -sine.T], [sine.T, cosine.T]]) / LENGTH
    lane_matrices = [*parts(forward), *parts(inverse)]
    return parity, block, lane_phase, np.stack(row_matrices), np.stack(lane_matrices)


def call(kernel, out_shape, scratch, *operands, scalars=0):
    return pl.pallas_call(
        kernel,
        out_shape=jax.ShapeDtypeStruct(*out_shape),
        in_specs=[pl.BlockSpec(memory_space=pltpu.SMEM)] * scalars
        + [pl.BlockSpec(memory_space=pltpu.VMEM)] * (len(operands) - scalars),
        out_specs=pl.BlockSpec(memory_space=pltpu.VMEM),
        scratch_shapes=[pltpu.VMEM(shape, F32) for shape in scratch],
        compiler_params=pltpu.CompilerParams(vmem_limit_bytes=VMEM_LIMIT),
    )(*operands)


def apply_filter(place, series, response, **kwargs):
    return call(
        filter_kernel,
        ((N_CTX, ROWS, LANES), BF16),
        [(HALF, ROWS, LANES), (HALF, 2 * ROWS, LANES)],
        place,
        series,
        response,
        *(jnp.asarray(table) for table in tables()),
        scalars=1,
        **kwargs,
    )


def exchange(x, axis):
    return lax.all_to_all(x, axis, split_axis=0, concat_axis=0, tiled=True)


def spread_spectra(blocks):
    for bit in (3, 2, 1, 0):
        shape = blocks.shape
        view = blocks.reshape(HALF >> (bit + 1), 2, 1 << bit, *shape[1:])
        pairs = [(device, device ^ (1 << bit)) for device in range(N_CTX)]
        there = lax.ppermute(view[:, 1], "ctx", pairs)
        blocks = jnp.stack([view[:, 0], there], axis=1).reshape(shape)
    return blocks


def body(value_branch, key_branch, gate_branch, skip_gain, spectra):
    device = lax.axis_index("ctx")
    place = jnp.stack([device & 15, device >> 4])

    packed = call(
        product_kernel, ((N_CHAN, 48, LANES), BF16), [(CHANNELS, TOKENS), (N_CHAN, 48, LANES)], key_branch, value_branch
    )
    packed, spectra = lax.optimization_barrier((packed, spectra))
    response = call(
        spectra_kernel,
        ((HALF, 2 * ROWS, LANES), BF16),
        [],
        place,
        spectra.reshape(2, GROUP, ROWS, LANES),
        scalars=1,
    )
    response = spread_spectra(response)
    gathered = exchange(packed, "chan")
    sent = call(fan_out_kernel, ((N_CTX, ROWS, LANES), BF16), [(N_CHAN * 48, LANES)], gathered)
    series = exchange(sent, "ctx")
    parts = exchange(apply_filter(place, series, response), "ctx")
    joined = call(join_kernel, ((N_CHAN, 48, LANES), BF16), [(N_CHAN * 48, LANES)], parts)
    tokens = exchange(joined, "chan")
    return call(
        gate_kernel,
        ((CHANNELS, TOKENS), BF16),
        [(N_CHAN, 48, LANES), (CHANNELS, TOKENS)],
        tokens,
        key_branch,
        value_branch,
        gate_branch,
        skip_gain[:, None],
    )


def solution(mesh):
    in_specs = (
        P(None, ("ctx", "chan")),
        P(None, ("ctx", "chan")),
        P(None, ("ctx", "chan")),
        P(),
        P(None, "chan", "ctx", None),
    )
    out_specs = P(None, ("ctx", "chan"))
    return jax.shard_map(body, mesh=mesh, in_specs=in_specs, out_specs=out_specs, check_vma=False)
```

```python
import math

import jax
import jax.numpy as jnp
import ml_dtypes
import numpy as np
from jax import lax
from jax.experimental import pallas as pl
from jax.experimental.pallas import tpu as pltpu
from jax.sharding import PartitionSpec as P

N_CTX = 32
N_CHAN = 16
CHANNELS = 192
GROUP = CHANNELS // N_CHAN
TOKENS = 512
SEQ = 8192
LENGTH = SEQ * N_CTX
LANES = 128
HALF = 16
CLASSES = 4
ROWS = SEQ // LANES
F32 = jnp.float32
BF16 = jnp.bfloat16
VMEM_LIMIT = 32 * 1024 * 1024


def rev4(number):
    return int(f"{number:04b}"[::-1], 2)


def c_root(a, turn, sign):
    if turn == 0:
        return a
    if turn == 0.25:
        return (-a[1], a[0]) if sign > 0 else (a[1], -a[0])
    cosine = math.cos(2 * math.pi * turn)
    sine = sign * math.sin(2 * math.pi * turn)
    return (a[0] * cosine - a[1] * sine, a[0] * sine + a[1] * cosine)


def c_mul(a, re, im):
    return (a[0] * re - a[1] * im, a[0] * im + a[1] * re)


def fft_list(terms, sign):
    size = len(terms)
    if size == 1:
        return terms
    even = fft_list(terms[0::2], sign)
    odd = fft_list(terms[1::2], sign)
    odd = [c_root(term, index / size, sign) for index, term in enumerate(odd)]
    return [(e[0] + o[0], e[1] + o[1]) for e, o in zip(even, odd)] + [
        (e[0] - o[0], e[1] - o[1]) for e, o in zip(even, odd)
    ]


def product_kernel(key_ref, value_ref, out_ref, flat, wide):
    for block in range(CHANNELS // 16):
        rows = slice(16 * block, 16 * block + 16)
        product = key_ref[rows, :].astype(F32) * value_ref[rows, :].astype(F32)
        flat[rows, :] = product
    for target in range(N_CHAN):
        for quarter in range(4):
            wide[target, GROUP * quarter : GROUP * quarter + GROUP, :] = flat[
                GROUP * target : GROUP * target + GROUP, LANES * quarter : LANES * quarter + LANES
            ]
    for target in range(N_CHAN):
        out_ref[target] = wide[target].astype(BF16)


def fan_out_kernel(in_ref, out_ref, wide):
    for source in range(N_CHAN):
        wide[48 * source : 48 * source + 48, :] = in_ref[source].astype(F32)
    for channel in range(GROUP):
        series = wide[pl.ds(channel, ROWS, stride=GROUP), :].astype(BF16)
        out_ref[channel] = series
        out_ref[HALF + channel] = series
    for channel in range(GROUP, HALF):
        empty = jnp.zeros((ROWS, LANES), BF16)
        out_ref[channel] = empty
        out_ref[HALF + channel] = empty


def join_kernel(in_ref, out_ref, wide):
    for channel in range(GROUP):
        total = in_ref[channel].astype(F32) + in_ref[HALF + channel].astype(F32)
        wide[pl.ds(channel, ROWS, stride=GROUP), :] = total
    for target in range(N_CHAN):
        out_ref[target] = wide[48 * target : 48 * target + 48, :].astype(BF16)


def gate_kernel(conv_ref, key_ref, value_ref, gate_ref, skip_ref, out_ref, wide, flat):
    for source in range(N_CHAN):
        wide[source] = conv_ref[source].astype(F32)
    for source in range(N_CHAN):
        for quarter in range(4):
            flat[GROUP * source : GROUP * source + GROUP, LANES * quarter : LANES * quarter + LANES] = wide[
                source, GROUP * quarter : GROUP * quarter + GROUP, :
            ]
    for block in range(CHANNELS // 16):
        rows = slice(16 * block, 16 * block + 16)
        carried = (key_ref[rows, :].astype(F32) * value_ref[rows, :].astype(F32)).astype(BF16).astype(F32)
        total = flat[rows, :] + skip_ref[rows, :] * carried
        out_ref[rows, :] = (gate_ref[rows, :].astype(F32) * total).astype(BF16)


def spectra_kernel(place_ref, in_ref, out_ref):
    place = place_ref[0]
    for channel in range(GROUP):
        distance = place ^ channel
        slot = (((distance >> 1) & 3) << 2) | ((distance >> 3) << 1) | (distance & 1)
        parts = []
        for part in range(2):
            turned = in_ref[part, channel].T
            parts.append(jnp.concatenate([turned[:64, :], turned[64:, :]], axis=1))
        out_ref[slot] = jnp.concatenate(parts, axis=0).astype(BF16)
    for channel in range(GROUP, HALF):
        distance = place ^ channel
        slot = (((distance >> 1) & 3) << 2) | ((distance >> 3) << 1) | (distance & 1)
        out_ref[slot] = jnp.zeros((2 * ROWS, LANES), BF16)


def split(x):
    high = x.astype(BF16)
    return high, (x - high.astype(F32)).astype(BF16)


def dot(a, b):
    return jnp.dot(a, b, preferred_element_type=F32)


def filter_kernel(
    place_ref, in_ref, spectra_ref, parity_ref, block_ref, lane_ref, row_matrix_ref, lane_matrix_ref, out_ref, real, pair
):
    place = place_ref[0]
    odd = place_ref[1]
    sign = jnp.where(odd == 0, 1.0, -1.0).astype(F32)

    def entry_phase(index, rows):
        cosine = jnp.where(odd == 0, 1.0, math.cos(math.pi * index / HALF)).astype(F32)
        sine = jnp.where(odd == 0, 0.0, -math.sin(math.pi * index / HALF)).astype(F32)
        re, im = parity_ref[0, rows, :], parity_ref[1, rows, :]
        re = jnp.where(odd == 0, 1.0, re)
        im = jnp.where(odd == 0, 0.0, im)
        return (re * cosine - im * sine, re * sine + im * cosine)

    for index in range(HALF):
        real[index] = in_ref[index].astype(F32) + sign * in_ref[HALF + index].astype(F32)
    for group in range(ROWS // 8):
        rows = slice(8 * group, 8 * group + 8)
        terms = []
        for index in range(HALF):
            phase = entry_phase(index, rows)
            term = real[index, rows, :]
            terms.append((term * phase[0], term * phase[1]))
        for kp, term in enumerate(fft_list(terms, -1)):
            if kp:
                term = c_mul(term, block_ref[0, kp, rows, :], block_ref[1, kp, rows, :])
            columns = slice(LANES * kp, LANES * kp + LANES)
            pair[8 * group : 8 * group + 8, columns] = term[0]
            pair[ROWS + 8 * group : ROWS + 8 * group + 8, columns] = term[1]
    lane_re, lane_im = lane_ref[0], lane_ref[1]
    for first in range(0, HALF, CLASSES):
        columns = slice(LANES * first, LANES * (first + CLASSES))
        high, low = split(pair[:, columns])
        mixed = dot(row_matrix_ref[0], jnp.concatenate([high, low, high], axis=0))
        turned = []
        for index in range(CLASSES):
            lanes = slice(LANES * index, LANES * index + LANES)
            term = c_mul((mixed[:ROWS, lanes], mixed[ROWS:, lanes]), lane_re, lane_im)
            turned.append(jnp.concatenate(term, axis=1))
        high, low = split(jnp.concatenate(turned, axis=0))
        spectrum = dot(jnp.concatenate([high, low, high], axis=1), lane_matrix_ref[0])
        shaped = []
        for index in range(CLASSES):
            rows = slice(ROWS * index, ROWS * index + ROWS)
            response = spectra_ref[slot_of(place ^ rev4(first + index))].astype(F32)
            term = c_mul((spectrum[rows, :LANES], spectrum[rows, LANES:]), response[:ROWS], response[ROWS:])
            shaped.append(jnp.concatenate(term, axis=1))
        high, low = split(jnp.concatenate(shaped, axis=0))
        mixed = dot(jnp.concatenate([high, low, high], axis=1), lane_matrix_ref[1])
        turned = []
        for index in range(CLASSES):
            rows = slice(ROWS * index, ROWS * index + ROWS)
            term = c_mul((mixed[rows, :LANES], mixed[rows, LANES:]), lane_re, -lane_im)
            turned.append(jnp.concatenate(term, axis=0))
        high, low = split(jnp.concatenate(turned, axis=1))
        pair[:, columns] = dot(row_matrix_ref[1], jnp.concatenate([high, low, high], axis=0))
    for group in range(ROWS // 8):
        rows = slice(8 * group, 8 * group + 8)
        terms = []
        for kp in range(HALF):
            columns = slice(LANES * kp, LANES * kp + LANES)
            term = (pair[8 * group : 8 * group + 8, columns], pair[ROWS + 8 * group : ROWS + 8 * group + 8, columns])
            if kp:
                term = c_mul(term, block_ref[0, kp, rows, :], -block_ref[1, kp, rows, :])
            terms.append(term)
        for index, term in enumerate(fft_list(terms, 1)):
            phase = entry_phase(index, rows)
            real[index, rows, :] = term[0] * phase[0] + term[1] * phase[1]
    for index in range(HALF):
        total = real[index]
        out_ref[index] = total.astype(BF16)
        out_ref[HALF + index] = (sign * total).astype(BF16)


def phases(numerator, denominator):
    angle = -2 * np.pi * (numerator % denominator) / denominator
    return np.cos(angle), np.sin(angle)


def tables():
    row, lane = np.arange(ROWS), np.arange(LANES)
    offset = (LANES * row[:, None] + lane[None, :])[None]
    kp = np.arange(HALF)[:, None, None]
    parity = np.stack(phases(offset[0], LENGTH)).astype(np.float32)
    block = np.stack(phases(2 * kp * offset, LENGTH)).astype(np.float32)
    lane_phase = np.stack(phases(row[:, None] * lane[None, :], SEQ)).astype(np.float32)

    def parts(matrix):
        high = matrix.astype(ml_dtypes.bfloat16)
        return high, (matrix - high.astype(np.float64)).astype(ml_dtypes.bfloat16)

    cosine, sine = phases(row[:, None] * row[None, :], ROWS)
    row_matrices = []
    for flip in (1, -1):
        high, low = parts(np.block([[cosine, -flip * sine], [flip * sine, cosine]]))
        row_matrices.append(np.concatenate([high, high, low], axis=1))
    order = np.concatenate([np.arange(0, LANES, 2), np.arange(1, LANES, 2)])
    cosine, sine = phases(lane[:, None] * order[None, :], LANES)
    forward = np.block([[cosine, sine], [-sine, cosine]])
    inverse = np.block([[cosine.T, -sine.T], [sine.T, cosine.T]]) / LENGTH
    lane_matrices = []
    for matrix in (forward, inverse):
        high, low = parts(matrix)
        lane_matrices.append(np.concatenate([high, high, low], axis=0))
    return parity, block, lane_phase, np.stack(row_matrices), np.stack(lane_matrices)


def call(kernel, out_shape, scratch, *operands, scalars=0):
    return pl.pallas_call(
        kernel,
        out_shape=jax.ShapeDtypeStruct(*out_shape),
        in_specs=[pl.BlockSpec(memory_space=pltpu.SMEM)] * scalars
        + [pl.BlockSpec(memory_space=pltpu.VMEM)] * (len(operands) - scalars),
        out_specs=pl.BlockSpec(memory_space=pltpu.VMEM),
        scratch_shapes=[pltpu.VMEM(shape, F32) for shape in scratch],
        compiler_params=pltpu.CompilerParams(vmem_limit_bytes=VMEM_LIMIT),
    )(*operands)


def apply_filter(place, series, response, **kwargs):
    return call(
        filter_kernel,
        ((N_CTX, ROWS, LANES), BF16),
        [(HALF, ROWS, LANES), (2 * ROWS, HALF * LANES)],
        place,
        series,
        response,
        *(jnp.asarray(table) for table in tables()),
        scalars=1,
        **kwargs,
    )


def exchange(x, axis):
    return lax.all_to_all(x, axis, split_axis=0, concat_axis=0, tiled=True)


def slot_of(distance):
    return ((distance >> 3) << 3) | ((distance & 1) << 2) | ((distance >> 1) & 3)


def swap(pieces, distances):
    there = [pieces[0]]
    for piece, distance in zip(pieces[1:], distances[1:]):
        there.append(lax.ppermute(piece, "ctx", [(device, device ^ distance) for device in range(N_CTX)]))
    return there


def spread_spectra(blocks):
    pieces = swap([blocks[4 * x : 4 * x + 4] for x in range(4)], (0, 2, 4, 6))
    pieces = swap([jnp.stack([piece[other] for piece in pieces]) for other in range(4)], (0, 1, 8, 9))
    return jnp.concatenate(pieces, axis=0)


def body(value_branch, key_branch, gate_branch, skip_gain, spectra):
    device = lax.axis_index("ctx")
    place = jnp.stack([device & 15, device >> 4])

    packed = call(
        product_kernel, ((N_CHAN, 48, LANES), BF16), [(CHANNELS, TOKENS), (N_CHAN, 48, LANES)], key_branch, value_branch
    )
    packed, spectra = lax.optimization_barrier((packed, spectra))
    response = call(
        spectra_kernel,
        ((HALF, 2 * ROWS, LANES), BF16),
        [],
        place,
        spectra.reshape(2, GROUP, ROWS, LANES),
        scalars=1,
    )
    response = spread_spectra(response)
    gathered = exchange(packed, "chan")
    sent = call(fan_out_kernel, ((N_CTX, ROWS, LANES), BF16), [(N_CHAN * 48, LANES)], gathered)
    series = exchange(sent, "ctx")
    parts = exchange(apply_filter(place, series, response), "ctx")
    joined = call(join_kernel, ((N_CHAN, 48, LANES), BF16), [(N_CHAN * 48, LANES)], parts)
    tokens = exchange(joined, "chan")
    return call(
        gate_kernel,
        ((CHANNELS, TOKENS), BF16),
        [(N_CHAN, 48, LANES), (CHANNELS, TOKENS)],
        tokens,
        key_branch,
        value_branch,
        gate_branch,
        skip_gain[:, None],
    )


def solution(mesh):
    in_specs = (
        P(None, ("ctx", "chan")),
        P(None, ("ctx", "chan")),
        P(None, ("ctx", "chan")),
        P(),
        P(None, "chan", "ctx", None),
    )
    out_specs = P(None, ("ctx", "chan"))
    return jax.shard_map(body, mesh=mesh, in_specs=in_specs, out_specs=out_specs, check_vma=False)
```

```python
import math

import jax
import jax.numpy as jnp
import ml_dtypes
import numpy as np
from jax import lax
from jax.experimental import pallas as pl
from jax.experimental.pallas import tpu as pltpu
from jax.sharding import PartitionSpec as P

N_CTX = 32
N_CHAN = 16
CHANNELS = 192
GROUP = CHANNELS // N_CHAN
TOKENS = 512
SEQ = 8192
LENGTH = SEQ * N_CTX
LANES = 128
HALF = 16
CLASSES = 4
ROWS = SEQ // LANES
F32 = jnp.float32
BF16 = jnp.bfloat16
VMEM_LIMIT = 32 * 1024 * 1024


def rev4(number):
    return int(f"{number:04b}"[::-1], 2)


def c_root(a, turn, sign):
    if turn == 0:
        return a
    if turn == 0.25:
        return (-a[1], a[0]) if sign > 0 else (a[1], -a[0])
    cosine = math.cos(2 * math.pi * turn)
    sine = sign * math.sin(2 * math.pi * turn)
    return (a[0] * cosine - a[1] * sine, a[0] * sine + a[1] * cosine)


def c_mul(a, re, im):
    return (a[0] * re - a[1] * im, a[0] * im + a[1] * re)


def fft_list(terms, sign):
    size = len(terms)
    if size == 1:
        return terms
    even = fft_list(terms[0::2], sign)
    odd = fft_list(terms[1::2], sign)
    odd = [c_root(term, index / size, sign) for index, term in enumerate(odd)]
    return [(e[0] + o[0], e[1] + o[1]) for e, o in zip(even, odd)] + [
        (e[0] - o[0], e[1] - o[1]) for e, o in zip(even, odd)
    ]


def product_kernel(key_ref, value_ref, out_ref, flat, wide):
    for block in range(CHANNELS // 16):
        rows = slice(16 * block, 16 * block + 16)
        product = key_ref[rows, :].astype(F32) * value_ref[rows, :].astype(F32)
        flat[rows, :] = product
    for target in range(N_CHAN):
        for quarter in range(4):
            wide[target, GROUP * quarter : GROUP * quarter + GROUP, :] = flat[
                GROUP * target : GROUP * target + GROUP, LANES * quarter : LANES * quarter + LANES
            ]
    for target in range(N_CHAN):
        out_ref[target] = wide[target].astype(BF16)


def fan_out_kernel(in_ref, out_ref, wide):
    for source in range(N_CHAN):
        wide[48 * source : 48 * source + 48, :] = in_ref[source].astype(F32)
    for channel in range(GROUP):
        series = wide[pl.ds(channel, ROWS, stride=GROUP), :].astype(BF16)
        out_ref[channel] = series
        out_ref[HALF + channel] = series
    for channel in range(GROUP, HALF):
        empty = jnp.zeros((ROWS, LANES), BF16)
        out_ref[channel] = empty
        out_ref[HALF + channel] = empty


def join_kernel(in_ref, out_ref, wide):
    for channel in range(GROUP):
        total = in_ref[channel].astype(F32) + in_ref[HALF + channel].astype(F32)
        wide[pl.ds(channel, ROWS, stride=GROUP), :] = total
    for target in range(N_CHAN):
        out_ref[target] = wide[48 * target : 48 * target + 48, :].astype(BF16)


def gate_kernel(conv_ref, key_ref, value_ref, gate_ref, skip_ref, out_ref, wide, flat):
    for source in range(N_CHAN):
        wide[source] = conv_ref[source].astype(F32)
    for source in range(N_CHAN):
        for quarter in range(4):
            flat[GROUP * source : GROUP * source + GROUP, LANES * quarter : LANES * quarter + LANES] = wide[
                source, GROUP * quarter : GROUP * quarter + GROUP, :
            ]
    for block in range(CHANNELS // 16):
        rows = slice(16 * block, 16 * block + 16)
        carried = (key_ref[rows, :].astype(F32) * value_ref[rows, :].astype(F32)).astype(BF16).astype(F32)
        total = flat[rows, :] + skip_ref[rows, :] * carried
        out_ref[rows, :] = (gate_ref[rows, :].astype(F32) * total).astype(BF16)


def spectra_kernel(in_ref, out_ref):
    for channel in range(GROUP):
        parts = []
        for part in range(2):
            turned = in_ref[part, channel].T
            parts.append(jnp.concatenate([turned[:64, :], turned[64:, :]], axis=1))
        out_ref[channel] = jnp.concatenate(parts, axis=0).astype(BF16)


def split(x):
    high = x.astype(BF16)
    return high, (x - high.astype(F32)).astype(BF16)


def dot(a, b):
    return jnp.dot(a, b, preferred_element_type=F32)


def filter_kernel(
    place_ref,
    in_ref,
    here_ref,
    there_ref,
    parity_ref,
    block_ref,
    lane_ref,
    row_matrix_ref,
    lane_matrix_ref,
    out_ref,
    real,
    pair,
):
    core = place_ref[0] & 1
    odd = place_ref[1]
    sign = jnp.where(odd == 0, 1.0, -1.0).astype(F32)

    def entry_phase(index, rows):
        cosine = jnp.where(odd == 0, 1.0, math.cos(math.pi * index / HALF)).astype(F32)
        sine = jnp.where(odd == 0, 0.0, -math.sin(math.pi * index / HALF)).astype(F32)
        re, im = parity_ref[0, rows, :], parity_ref[1, rows, :]
        re = jnp.where(odd == 0, 1.0, re)
        im = jnp.where(odd == 0, 0.0, im)
        return (re * cosine - im * sine, re * sine + im * cosine)

    for index in range(HALF):
        real[index] = in_ref[index].astype(F32) + sign * in_ref[HALF + index].astype(F32)
    for group in range(ROWS // 8):
        rows = slice(8 * group, 8 * group + 8)
        terms = []
        for index in range(HALF):
            phase = entry_phase(index, rows)
            term = real[index, rows, :]
            terms.append((term * phase[0], term * phase[1]))
        for kp, term in enumerate(fft_list(terms, -1)):
            if kp:
                term = c_mul(term, block_ref[0, kp, rows, :], block_ref[1, kp, rows, :])
            columns = slice(LANES * kp, LANES * kp + LANES)
            pair[8 * group : 8 * group + 8, columns] = term[0]
            pair[ROWS + 8 * group : ROWS + 8 * group + 8, columns] = term[1]
    lane_re, lane_im = lane_ref[0], lane_ref[1]
    for first in range(0, HALF, CLASSES):
        columns = slice(LANES * first, LANES * (first + CLASSES))
        high, low = split(pair[:, columns])
        mixed = dot(row_matrix_ref[0], jnp.concatenate([high, low, high], axis=0))
        turned = []
        for index in range(CLASSES):
            lanes = slice(LANES * index, LANES * index + LANES)
            term = c_mul((mixed[:ROWS, lanes], mixed[ROWS:, lanes]), lane_re, lane_im)
            turned.append(jnp.concatenate(term, axis=1))
        high, low = split(jnp.concatenate(turned, axis=0))
        spectrum = dot(jnp.concatenate([high, low, high], axis=1), lane_matrix_ref[0])
        shaped = []
        for index in range(CLASSES):
            rows = slice(ROWS * index, ROWS * index + ROWS)
            source = rev4(first + index)
            response = jnp.where(core == source % 2, here_ref[source // 2], there_ref[source // 2]).astype(F32)
            term = c_mul((spectrum[rows, :LANES], spectrum[rows, LANES:]), response[:ROWS], response[ROWS:])
            shaped.append(jnp.concatenate(term, axis=1))
        high, low = split(jnp.concatenate(shaped, axis=0))
        mixed = dot(jnp.concatenate([high, low, high], axis=1), lane_matrix_ref[1])
        turned = []
        for index in range(CLASSES):
            rows = slice(ROWS * index, ROWS * index + ROWS)
            term = c_mul((mixed[rows, :LANES], mixed[rows, LANES:]), lane_re, -lane_im)
            turned.append(jnp.concatenate(term, axis=0))
        high, low = split(jnp.concatenate(turned, axis=1))
        pair[:, columns] = dot(row_matrix_ref[1], jnp.concatenate([high, low, high], axis=0))
    for group in range(ROWS // 8):
        rows = slice(8 * group, 8 * group + 8)
        terms = []
        for kp in range(HALF):
            columns = slice(LANES * kp, LANES * kp + LANES)
            term = (pair[8 * group : 8 * group + 8, columns], pair[ROWS + 8 * group : ROWS + 8 * group + 8, columns])
            if kp:
                term = c_mul(term, block_ref[0, kp, rows, :], -block_ref[1, kp, rows, :])
            terms.append(term)
        for index, term in enumerate(fft_list(terms, 1)):
            phase = entry_phase(index, rows)
            real[index, rows, :] = term[0] * phase[0] + term[1] * phase[1]
    for index in range(HALF):
        total = real[index]
        out_ref[index] = total.astype(BF16)
        out_ref[HALF + index] = (sign * total).astype(BF16)


def phases(numerator, denominator):
    angle = -2 * np.pi * (numerator % denominator) / denominator
    return np.cos(angle), np.sin(angle)


def tables():
    row, lane = np.arange(ROWS), np.arange(LANES)
    offset = (LANES * row[:, None] + lane[None, :])[None]
    kp = np.arange(HALF)[:, None, None]
    parity = np.stack(phases(offset[0], LENGTH)).astype(np.float32)
    block = np.stack(phases(2 * kp * offset, LENGTH)).astype(np.float32)
    lane_phase = np.stack(phases(row[:, None] * lane[None, :], SEQ)).astype(np.float32)

    def parts(matrix):
        high = matrix.astype(ml_dtypes.bfloat16)
        return high, (matrix - high.astype(np.float64)).astype(ml_dtypes.bfloat16)

    cosine, sine = phases(row[:, None] * row[None, :], ROWS)
    row_matrices = []
    for flip in (1, -1):
        high, low = parts(np.block([[cosine, -flip * sine], [flip * sine, cosine]]))
        row_matrices.append(np.concatenate([high, high, low], axis=1))
    order = np.concatenate([np.arange(0, LANES, 2), np.arange(1, LANES, 2)])
    cosine, sine = phases(lane[:, None] * order[None, :], LANES)
    forward = np.block([[cosine, sine], [-sine, cosine]])
    inverse = np.block([[cosine.T, -sine.T], [sine.T, cosine.T]]) / LENGTH
    lane_matrices = []
    for matrix in (forward, inverse):
        high, low = parts(matrix)
        lane_matrices.append(np.concatenate([high, high, low], axis=0))
    return parity, block, lane_phase, np.stack(row_matrices), np.stack(lane_matrices)


def call(kernel, out_shape, scratch, *operands, scalars=0):
    return pl.pallas_call(
        kernel,
        out_shape=jax.ShapeDtypeStruct(*out_shape),
        in_specs=[pl.BlockSpec(memory_space=pltpu.SMEM)] * scalars
        + [pl.BlockSpec(memory_space=pltpu.VMEM)] * (len(operands) - scalars),
        out_specs=pl.BlockSpec(memory_space=pltpu.VMEM),
        scratch_shapes=[pltpu.VMEM(shape, F32) for shape in scratch],
        compiler_params=pltpu.CompilerParams(vmem_limit_bytes=VMEM_LIMIT),
    )(*operands)


def apply_filter(place, series, response):
    return call(
        filter_kernel,
        ((N_CTX, ROWS, LANES), BF16),
        [(HALF, ROWS, LANES), (2 * ROWS, HALF * LANES)],
        place,
        series,
        *response,
        *(jnp.asarray(table) for table in tables()),
        scalars=1,
    )


def exchange(x, axis):
    return lax.all_to_all(x, axis, split_axis=0, concat_axis=0, tiled=True)


def spread_spectra(blocks, place):
    equal_core = [[16 * half + 2 * chip + core for chip in range(8)] for half in range(2) for core in range(2)]
    blocks = lax.all_gather(blocks, "ctx", axis_index_groups=equal_core)
    here = lax.dynamic_index_in_dim(blocks, place[0], 1, keepdims=False)
    there = lax.dynamic_index_in_dim(blocks, place[0] ^ 1, 1, keepdims=False)
    there = lax.ppermute(there, "ctx", [(device, device ^ 1) for device in range(N_CTX)])
    return here, there


def body(value_branch, key_branch, gate_branch, skip_gain, spectra):
    device = lax.axis_index("ctx")
    place = jnp.stack([device & 15, device >> 4])

    packed = call(
        product_kernel, ((N_CHAN, 48, LANES), BF16), [(CHANNELS, TOKENS), (N_CHAN, 48, LANES)], key_branch, value_branch
    )
    packed, spectra = lax.optimization_barrier((packed, spectra))
    response = call(
        spectra_kernel, ((GROUP, 2 * ROWS, LANES), BF16), [], spectra.reshape(2, GROUP, ROWS, LANES)
    )
    response = spread_spectra(response, place)
    gathered = exchange(packed, "chan")
    sent = call(fan_out_kernel, ((N_CTX, ROWS, LANES), BF16), [(N_CHAN * 48, LANES)], gathered)
    series = exchange(sent, "ctx")
    parts = exchange(apply_filter(place, series, response), "ctx")
    joined = call(join_kernel, ((N_CHAN, 48, LANES), BF16), [(N_CHAN * 48, LANES)], parts)
    tokens = exchange(joined, "chan")
    return call(
        gate_kernel,
        ((CHANNELS, TOKENS), BF16),
        [(N_CHAN, 48, LANES), (CHANNELS, TOKENS)],
        tokens,
        key_branch,
        value_branch,
        gate_branch,
        skip_gain[:, None],
    )


def solution(mesh):
    in_specs = (
        P(None, ("ctx", "chan")),
        P(None, ("ctx", "chan")),
        P(None, ("ctx", "chan")),
        P(),
        P(None, "chan", "ctx", None),
    )
    out_specs = P(None, ("ctx", "chan"))
    return jax.shard_map(body, mesh=mesh, in_specs=in_specs, out_specs=out_specs, check_vma=False)
```

```python
import math

import jax
import jax.numpy as jnp
import ml_dtypes
import numpy as np
from jax import lax
from jax.experimental import pallas as pl
from jax.experimental.pallas import tpu as pltpu
from jax.sharding import PartitionSpec as P

N_CTX = 32
N_CHAN = 16
CHANNELS = 192
GROUP = CHANNELS // N_CHAN
TOKENS = 512
SEQ = 8192
LENGTH = SEQ * N_CTX
LANES = 128
HALF = 16
CLASSES = 4
ROWS = SEQ // LANES
F32 = jnp.float32
BF16 = jnp.bfloat16
VMEM_LIMIT = 32 * 1024 * 1024


def rev4(number):
    return int(f"{number:04b}"[::-1], 2)


def c_root(a, turn, sign):
    if turn == 0:
        return a
    if turn == 0.25:
        return (-a[1], a[0]) if sign > 0 else (a[1], -a[0])
    cosine = math.cos(2 * math.pi * turn)
    sine = sign * math.sin(2 * math.pi * turn)
    return (a[0] * cosine - a[1] * sine, a[0] * sine + a[1] * cosine)


def c_mul(a, re, im):
    return (a[0] * re - a[1] * im, a[0] * im + a[1] * re)


def fft_list(terms, sign):
    size = len(terms)
    if size == 1:
        return terms
    even = fft_list(terms[0::2], sign)
    odd = fft_list(terms[1::2], sign)
    odd = [c_root(term, index / size, sign) for index, term in enumerate(odd)]
    return [(e[0] + o[0], e[1] + o[1]) for e, o in zip(even, odd)] + [
        (e[0] - o[0], e[1] - o[1]) for e, o in zip(even, odd)
    ]


def pack_kernel(key_ref, value_ref, out_ref, wide):
    low = lax.broadcasted_iota(jnp.int32, (8, LANES), 0) < 4
    for block in range(CHANNELS // 16):
        rows = slice(16 * block, 16 * block + 16)
        carried = (key_ref[rows, :].astype(F32) * value_ref[rows, :].astype(F32)).astype(BF16).astype(F32)
        for part in range(2):
            for upper in range(2):
                a = carried[8 * part : 8 * part + 8, 256 * upper : 256 * upper + 128]
                b = carried[8 * part : 8 * part + 8, 256 * upper + 128 : 256 * upper + 256]
                first = jnp.where(low, a, pltpu.roll(b, 4, 0))
                second = jnp.where(low, pltpu.roll(a, 4, 0), b)
                for offset, piece in enumerate((first, second)):
                    quad = 4 * block + 2 * part + offset
                    start = 24 * upper + 8 * (quad % 3)
                    wide[quad // 3, start : start + 8, :] = piece
    for target in range(N_CHAN):
        out_ref[target] = wide[target].astype(BF16)


def gate_kernel(conv_ref, key_ref, value_ref, gate_ref, skip_ref, out_ref, wide, flat):
    low = lax.broadcasted_iota(jnp.int32, (8, LANES), 0) < 4
    for source in range(N_CHAN):
        wide[source] = conv_ref[source].astype(F32)
    for block in range(CHANNELS // 8):
        for upper in range(2):
            pieces = []
            for offset in range(2):
                quad = 2 * block + offset
                start = 24 * upper + 8 * (quad % 3)
                pieces.append(wide[quad // 3, start : start + 8, :])
            first, second = pieces
            flat[8 * block : 8 * block + 8, 256 * upper : 256 * upper + 128] = jnp.where(
                low, first, pltpu.roll(second, 4, 0)
            )
            flat[8 * block : 8 * block + 8, 256 * upper + 128 : 256 * upper + 256] = jnp.where(
                low, pltpu.roll(first, 4, 0), second
            )
    for block in range(CHANNELS // 16):
        rows = slice(16 * block, 16 * block + 16)
        carried = (key_ref[rows, :].astype(F32) * value_ref[rows, :].astype(F32)).astype(BF16).astype(F32)
        total = flat[rows, :] + skip_ref[rows, :] * carried
        out_ref[rows, :] = (gate_ref[rows, :].astype(F32) * total).astype(BF16)


def fan_out_kernel(in_ref, blocks_ref, out_ref, wide):
    for source in range(N_CHAN):
        wide[48 * source : 48 * source + 48, :] = in_ref[source].astype(F32)
    for channel in range(GROUP):
        first = 8 * (channel // 4) + channel % 4
        pieces = [wide[pl.ds(first + 4 * quarter, ROWS // 2, stride=24), :] for quarter in range(2)]
        series = jnp.concatenate(pieces, axis=0).astype(BF16)
        block = blocks_ref[channel]
        for parity in range(2):
            out_ref[HALF * parity + channel, 0:ROWS, :] = series
            out_ref[HALF * parity + channel, ROWS : 3 * ROWS, :] = block
    for channel in range(GROUP, HALF):
        for parity in range(2):
            out_ref[HALF * parity + channel] = jnp.zeros((3 * ROWS, LANES), BF16)


def join_kernel(in_ref, out_ref, wide):
    for channel in range(GROUP):
        total = in_ref[channel].astype(F32) + in_ref[HALF + channel].astype(F32)
        first = 8 * (channel // 4) + channel % 4
        for quarter in range(2):
            wide[pl.ds(first + 4 * quarter, ROWS // 2, stride=24), :] = total[
                ROWS // 2 * quarter : ROWS // 2 * quarter + ROWS // 2
            ]
    for target in range(N_CHAN):
        out_ref[target] = wide[48 * target : 48 * target + 48, :].astype(BF16)


def spectra_kernel(in_ref, out_ref):
    for channel in range(GROUP):
        parts = []
        for part in range(2):
            turned = in_ref[part, channel].T
            parts.append(jnp.concatenate([turned[:64, :], turned[64:, :]], axis=1))
        out_ref[channel] = jnp.concatenate(parts, axis=0).astype(BF16)


def split(x):
    high = x.astype(BF16)
    return high, (x - high.astype(F32)).astype(BF16)


def dot(a, b):
    return jnp.dot(a, b, preferred_element_type=F32)


def filter_kernel(
    odd_ref, in_ref, parity_ref, block_ref, lane_ref, row_matrix_ref, lane_matrix_ref, out_ref, real, pair
):
    odd = odd_ref[0]
    sign = jnp.where(odd == 0, 1.0, -1.0).astype(F32)

    def entry_phase(index, rows):
        cosine = jnp.where(odd == 0, 1.0, math.cos(math.pi * index / HALF)).astype(F32)
        sine = jnp.where(odd == 0, 0.0, -math.sin(math.pi * index / HALF)).astype(F32)
        re, im = parity_ref[0, rows, :], parity_ref[1, rows, :]
        re = jnp.where(odd == 0, 1.0, re)
        im = jnp.where(odd == 0, 0.0, im)
        return (re * cosine - im * sine, re * sine + im * cosine)

    for index in range(HALF):
        real[index] = in_ref[index, 0:ROWS, :].astype(F32) + sign * in_ref[HALF + index, 0:ROWS, :].astype(F32)
    for group in range(ROWS // 8):
        rows = slice(8 * group, 8 * group + 8)
        terms = []
        for index in range(HALF):
            phase = entry_phase(index, rows)
            term = real[index, rows, :]
            terms.append((term * phase[0], term * phase[1]))
        for kp, term in enumerate(fft_list(terms, -1)):
            if kp:
                term = c_mul(term, block_ref[0, kp, rows, :], block_ref[1, kp, rows, :])
            columns = slice(LANES * kp, LANES * kp + LANES)
            pair[8 * group : 8 * group + 8, columns] = term[0]
            pair[ROWS + 8 * group : ROWS + 8 * group + 8, columns] = term[1]
    lane_re, lane_im = lane_ref[0], lane_ref[1]
    for first in range(0, HALF, CLASSES):
        columns = slice(LANES * first, LANES * (first + CLASSES))
        high, low = split(pair[:, columns])
        mixed = dot(row_matrix_ref[0], jnp.concatenate([high, low, high], axis=0))
        turned = []
        for index in range(CLASSES):
            lanes = slice(LANES * index, LANES * index + LANES)
            term = c_mul((mixed[:ROWS, lanes], mixed[ROWS:, lanes]), lane_re, lane_im)
            turned.append(jnp.concatenate(term, axis=1))
        high, low = split(jnp.concatenate(turned, axis=0))
        spectrum = dot(jnp.concatenate([high, low, high], axis=1), lane_matrix_ref[0])
        shaped = []
        for index in range(CLASSES):
            rows = slice(ROWS * index, ROWS * index + ROWS)
            response = in_ref[HALF * odd + rev4(first + index), ROWS : 3 * ROWS, :].astype(F32)
            term = c_mul((spectrum[rows, :LANES], spectrum[rows, LANES:]), response[:ROWS], response[ROWS:])
            shaped.append(jnp.concatenate(term, axis=1))
        high, low = split(jnp.concatenate(shaped, axis=0))
        mixed = dot(jnp.concatenate([high, low, high], axis=1), lane_matrix_ref[1])
        turned = []
        for index in range(CLASSES):
            rows = slice(ROWS * index, ROWS * index + ROWS)
            term = c_mul((mixed[rows, :LANES], mixed[rows, LANES:]), lane_re, -lane_im)
            turned.append(jnp.concatenate(term, axis=0))
        high, low = split(jnp.concatenate(turned, axis=1))
        pair[:, columns] = dot(row_matrix_ref[1], jnp.concatenate([high, low, high], axis=0))
    for group in range(ROWS // 8):
        rows = slice(8 * group, 8 * group + 8)
        terms = []
        for kp in range(HALF):
            columns = slice(LANES * kp, LANES * kp + LANES)
            term = (pair[8 * group : 8 * group + 8, columns], pair[ROWS + 8 * group : ROWS + 8 * group + 8, columns])
            if kp:
                term = c_mul(term, block_ref[0, kp, rows, :], -block_ref[1, kp, rows, :])
            terms.append(term)
        for index, term in enumerate(fft_list(terms, 1)):
            phase = entry_phase(index, rows)
            real[index, rows, :] = term[0] * phase[0] + term[1] * phase[1]
    for index in range(HALF):
        total = real[index]
        out_ref[index] = total.astype(BF16)
        out_ref[HALF + index] = (sign * total).astype(BF16)


def phases(numerator, denominator):
    angle = -2 * np.pi * (numerator % denominator) / denominator
    return np.cos(angle), np.sin(angle)


def row_order():
    pair = np.arange(ROWS // 2)
    return np.concatenate([2 * pair, 2 * pair + 1])


def tables():
    row, lane, order = np.arange(ROWS), np.arange(LANES), row_order()
    offset = (LANES * order[:, None] + lane[None, :])[None]
    kp = np.arange(HALF)[:, None, None]
    parity = np.stack(phases(offset[0], LENGTH)).astype(np.float32)
    block = np.stack(phases(2 * kp * offset, LENGTH)).astype(np.float32)
    lane_phase = np.stack(phases(row[:, None] * lane[None, :], SEQ)).astype(np.float32)

    def parts(matrix):
        high = matrix.astype(ml_dtypes.bfloat16)
        return high, (matrix - high.astype(np.float64)).astype(ml_dtypes.bfloat16)

    cosine, sine = phases(row[:, None] * order[None, :], ROWS)
    row_matrices = []
    for matrix in (np.block([[cosine, -sine], [sine, cosine]]), np.block([[cosine.T, sine.T], [-sine.T, cosine.T]])):
        high, low = parts(matrix)
        row_matrices.append(np.concatenate([high, high, low], axis=1))
    order = np.concatenate([np.arange(0, LANES, 2), np.arange(1, LANES, 2)])
    cosine, sine = phases(lane[:, None] * order[None, :], LANES)
    forward = np.block([[cosine, sine], [-sine, cosine]])
    inverse = np.block([[cosine.T, -sine.T], [sine.T, cosine.T]]) / LENGTH
    lane_matrices = []
    for matrix in (forward, inverse):
        high, low = parts(matrix)
        lane_matrices.append(np.concatenate([high, high, low], axis=0))
    return parity, block, lane_phase, np.stack(row_matrices), np.stack(lane_matrices)


def call(kernel, out_shape, scratch, *operands, scalars=0):
    return pl.pallas_call(
        kernel,
        out_shape=jax.ShapeDtypeStruct(*out_shape),
        in_specs=[pl.BlockSpec(memory_space=pltpu.SMEM)] * scalars
        + [pl.BlockSpec(memory_space=pltpu.VMEM)] * (len(operands) - scalars),
        out_specs=pl.BlockSpec(memory_space=pltpu.VMEM),
        scratch_shapes=[pltpu.VMEM(shape, F32) for shape in scratch],
        compiler_params=pltpu.CompilerParams(vmem_limit_bytes=VMEM_LIMIT),
    )(*operands)


def apply_filter(odd, received):
    return call(
        filter_kernel,
        ((N_CTX, ROWS, LANES), BF16),
        [(HALF, ROWS, LANES), (2 * ROWS, HALF * LANES)],
        odd,
        received,
        *(jnp.asarray(table) for table in tables()),
        scalars=1,
    )


def exchange(x, axis):
    return lax.all_to_all(x, axis, split_axis=0, concat_axis=0, tiled=True)


def body(value_branch, key_branch, gate_branch, skip_gain, spectra):
    odd = (lax.axis_index("ctx") >> 4)[None]
    packed = call(pack_kernel, ((N_CHAN, 48, LANES), BF16), [(N_CHAN, 48, LANES)], key_branch, value_branch)
    blocks = call(spectra_kernel, ((GROUP, 2 * ROWS, LANES), BF16), [], spectra.reshape(2, GROUP, ROWS, LANES))
    gathered = exchange(packed, "chan")
    sent = call(fan_out_kernel, ((N_CTX, 3 * ROWS, LANES), BF16), [(N_CHAN * 48, LANES)], gathered, blocks)
    received = exchange(sent, "ctx")
    parts = exchange(apply_filter(odd, received), "ctx")
    joined = call(join_kernel, ((N_CHAN, 48, LANES), BF16), [(N_CHAN * 48, LANES)], parts)
    tokens = exchange(joined, "chan")
    return call(
        gate_kernel,
        ((CHANNELS, TOKENS), BF16),
        [(N_CHAN, 48, LANES), (CHANNELS, TOKENS)],
        tokens,
        key_branch,
        value_branch,
        gate_branch,
        skip_gain[:, None],
    )


def solution(mesh):
    in_specs = (
        P(None, ("ctx", "chan")),
        P(None, ("ctx", "chan")),
        P(None, ("ctx", "chan")),
        P(),
        P(None, "chan", "ctx", None),
    )
    out_specs = P(None, ("ctx", "chan"))
    return jax.shard_map(body, mesh=mesh, in_specs=in_specs, out_specs=out_specs, check_vma=False)
```

```python
import math

import jax
import jax.numpy as jnp
import ml_dtypes
import numpy as np
from jax import lax
from jax.experimental import pallas as pl
from jax.experimental.pallas import tpu as pltpu
from jax.sharding import PartitionSpec as P

N_CTX = 32
N_CHAN = 16
CHANNELS = 192
GROUP = CHANNELS // N_CHAN
TOKENS = 512
SEQ = 8192
LENGTH = SEQ * N_CTX
LANES = 128
HALF = 16
CLASSES = 8
ROWS = SEQ // LANES
WORK = ROWS // 2
CHIPS = [chip for chip in range(HALF) if (chip + chip // 4) % 4 != 3]
F32 = jnp.float32
BF16 = jnp.bfloat16
VMEM_LIMIT = 32 * 1024 * 1024


def rev5(number):
    return int(f"{number:05b}"[::-1], 2)


def c_root(a, turn, sign):
    if turn == 0:
        return a
    if turn == 0.25:
        return (-a[1], a[0]) if sign > 0 else (a[1], -a[0])
    cosine = math.cos(2 * math.pi * turn)
    sine = sign * math.sin(2 * math.pi * turn)
    return (a[0] * cosine - a[1] * sine, a[0] * sine + a[1] * cosine)


def c_mul(a, re, im):
    return (a[0] * re - a[1] * im, a[0] * im + a[1] * re)


def fft_list(terms, sign):
    size = len(terms)
    if size == 1:
        return terms
    even = fft_list(terms[0::2], sign)
    odd = fft_list(terms[1::2], sign)
    odd = [c_root(term, index / size, sign) for index, term in enumerate(odd)]
    return [(e[0] + o[0], e[1] + o[1]) for e, o in zip(even, odd)] + [
        (e[0] - o[0], e[1] - o[1]) for e, o in zip(even, odd)
    ]


def pack_kernel(key_ref, value_ref, out_ref, wide):
    low = lax.broadcasted_iota(jnp.int32, (8, LANES), 0) < 4
    for block in range(CHANNELS // 16):
        rows = slice(16 * block, 16 * block + 16)
        carried = (key_ref[rows, :].astype(F32) * value_ref[rows, :].astype(F32)).astype(BF16).astype(F32)
        for part in range(2):
            for upper in range(2):
                a = carried[8 * part : 8 * part + 8, 256 * upper : 256 * upper + 128]
                b = carried[8 * part : 8 * part + 8, 256 * upper + 128 : 256 * upper + 256]
                first = jnp.where(low, a, pltpu.roll(b, 4, 0))
                second = jnp.where(low, pltpu.roll(a, 4, 0), b)
                for offset, piece in enumerate((first, second)):
                    quad = 4 * block + 2 * part + offset
                    start = 24 * upper + 8 * (quad % 3)
                    wide[quad // 3, start : start + 8, :] = piece
    for target in range(N_CHAN):
        out_ref[target] = wide[target].astype(BF16)


def gate_kernel(conv_ref, key_ref, value_ref, gate_ref, skip_ref, out_ref, wide, flat):
    low = lax.broadcasted_iota(jnp.int32, (8, LANES), 0) < 4
    for source in range(N_CHAN):
        wide[source] = conv_ref[source].astype(F32)
    for block in range(CHANNELS // 8):
        for upper in range(2):
            pieces = []
            for offset in range(2):
                quad = 2 * block + offset
                start = 24 * upper + 8 * (quad % 3)
                pieces.append(wide[quad // 3, start : start + 8, :])
            first, second = pieces
            flat[8 * block : 8 * block + 8, 256 * upper : 256 * upper + 128] = jnp.where(
                low, first, pltpu.roll(second, 4, 0)
            )
            flat[8 * block : 8 * block + 8, 256 * upper + 128 : 256 * upper + 256] = jnp.where(
                low, pltpu.roll(first, 4, 0), second
            )
    for block in range(CHANNELS // 16):
        rows = slice(16 * block, 16 * block + 16)
        carried = (key_ref[rows, :].astype(F32) * value_ref[rows, :].astype(F32)).astype(BF16).astype(F32)
        total = flat[rows, :] + skip_ref[rows, :] * carried
        out_ref[rows, :] = (gate_ref[rows, :].astype(F32) * total).astype(BF16)


def fan_out_kernel(in_ref, blocks_ref, out_ref, wide):
    for source in range(N_CHAN):
        wide[48 * source : 48 * source + 48, :] = in_ref[source].astype(F32)
    for channel, chip in enumerate(CHIPS):
        first = 8 * (channel // 4) + channel % 4
        pieces = [wide[pl.ds(first + 4 * quarter, ROWS // 2, stride=24), :] for quarter in range(2)]
        series = jnp.concatenate(pieces, axis=0).astype(BF16)
        for core in range(2):
            out_ref[2 * chip + core, 0:ROWS, :] = series
            out_ref[2 * chip + core, ROWS : 2 * ROWS, :] = blocks_ref[2 * channel + core]
    for chip in range(HALF):
        if chip not in CHIPS:
            for core in range(2):
                out_ref[2 * chip + core] = jnp.zeros((2 * ROWS, LANES), BF16)


def join_kernel(in_ref, out_ref, wide):
    for channel, chip in enumerate(CHIPS):
        total = in_ref[2 * chip].astype(F32) + in_ref[2 * chip + 1].astype(F32)
        first = 8 * (channel // 4) + channel % 4
        for quarter in range(2):
            wide[pl.ds(first + 4 * quarter, ROWS // 2, stride=24), :] = total[
                ROWS // 2 * quarter : ROWS // 2 * quarter + ROWS // 2
            ]
    for target in range(N_CHAN):
        out_ref[target] = wide[48 * target : 48 * target + 48, :].astype(BF16)


def spectra_kernel(in_ref, out_ref, turned):
    for channel in range(GROUP):
        for part in range(2):
            turned[LANES * part : LANES * part + LANES, :] = in_ref[part, channel].T
        for core in range(2):
            parts = []
            for part in range(2):
                starts = [LANES * part + 64 * upper + core for upper in range(2)]
                halves = [turned[pl.ds(start, 32, stride=2), :] for start in starts]
                parts.append(jnp.concatenate(halves, axis=1))
            out_ref[2 * channel + core] = jnp.concatenate(parts, axis=0).astype(BF16)


def split(x):
    high = x.astype(BF16)
    return high, (x - high.astype(F32)).astype(BF16)


def dot(a, b):
    return jnp.dot(a, b, preferred_element_type=F32)


def filter_kernel(core_ref, in_ref, block_ref, lane_ref, row_matrix_ref, lane_matrix_ref, out_ref, real, pair):
    sign = jnp.where(core_ref[0] == 0, 1.0, -1.0).astype(F32)
    for index in range(N_CTX):
        real[index] = in_ref[index, 0:ROWS, :].astype(F32)

    def places(group):
        start = 32 * (group // 2) + 8 * (group % 2)
        return slice(start, start + 8), slice(start + 16, start + 24), 8 * group

    for group in range(WORK // 8):
        early, late, row = places(group)
        sums = fft_list([(real[p, early, :], sign * real[p, late, :]) for p in range(N_CTX)], -1)
        for residue in range(N_CTX):
            here, mirror = sums[residue], sums[-residue % N_CTX]
            first = (here[0] + mirror[0], here[1] - mirror[1])
            second = (here[1] + mirror[1], mirror[0] - here[0])
            second = c_root(second, residue / 64, -1)
            term = (first[0] + second[0], first[1] + second[1])
            rows = slice(row, row + 8)
            term = c_mul(term, block_ref[0, residue, rows, :], block_ref[1, residue, rows, :])
            columns = slice(LANES * residue, LANES * residue + LANES)
            pair[row : row + 8, columns] = term[0]
            pair[WORK + row : WORK + row + 8, columns] = term[1]
    lane_re, lane_im = lane_ref[0], lane_ref[1]
    for first in range(0, N_CTX, CLASSES):
        columns = slice(LANES * first, LANES * (first + CLASSES))
        high, low = split(pair[:, columns])
        mixed = dot(row_matrix_ref[0], jnp.concatenate([high, low, high], axis=0))
        turned = []
        for index in range(CLASSES):
            lanes = slice(LANES * index, LANES * index + LANES)
            term = c_mul((mixed[:WORK, lanes], mixed[WORK:, lanes]), lane_re, lane_im)
            turned.append(jnp.concatenate(term, axis=1))
        high, low = split(jnp.concatenate(turned, axis=0))
        spectrum = dot(jnp.concatenate([high, low, high], axis=1), lane_matrix_ref[0])
        shaped = []
        for index in range(CLASSES):
            rows = slice(WORK * index, WORK * index + WORK)
            response = in_ref[rev5(first + index), ROWS : 2 * ROWS, :].astype(F32)
            term = c_mul((spectrum[rows, :LANES], spectrum[rows, LANES:]), response[:WORK], response[WORK:])
            shaped.append(jnp.concatenate(term, axis=1))
        high, low = split(jnp.concatenate(shaped, axis=0))
        mixed = dot(jnp.concatenate([high, low, high], axis=1), lane_matrix_ref[1])
        turned = []
        for index in range(CLASSES):
            rows = slice(WORK * index, WORK * index + WORK)
            term = c_mul((mixed[rows, :LANES], mixed[rows, LANES:]), lane_re, -lane_im)
            turned.append(jnp.concatenate(term, axis=0))
        high, low = split(jnp.concatenate(turned, axis=1))
        pair[:, columns] = dot(row_matrix_ref[1], jnp.concatenate([high, low, high], axis=0))
    for group in range(WORK // 8):
        early, late, row = places(group)
        rows = slice(row, row + 8)
        evens, odds = [], []
        for residue in range(N_CTX):
            columns = slice(LANES * residue, LANES * residue + LANES)
            term = (pair[row : row + 8, columns], pair[WORK + row : WORK + row + 8, columns])
            term = c_mul(term, block_ref[0, residue, rows, :], -block_ref[1, residue, rows, :])
            evens.append(term)
            odds.append(c_root(term, residue / 64, 1))
        terms = []
        for residue in range(N_CTX):
            mirror = -residue % N_CTX
            even = (evens[residue][0] + evens[mirror][0], evens[residue][1] - evens[mirror][1])
            odd = (odds[residue][0] + odds[mirror][0], odds[residue][1] - odds[mirror][1])
            terms.append((even[0] - odd[1], even[1] + odd[0]))
        for p, term in enumerate(fft_list(terms, 1)):
            real[p, early, :] = term[0]
            real[p, late, :] = sign * term[1]
    for index in range(N_CTX):
        out_ref[index] = real[index].astype(BF16)


def phases(numerator, denominator):
    angle = -2 * np.pi * (numerator % denominator) / denominator
    return np.cos(angle), np.sin(angle)


def row_order():
    pair = np.arange(ROWS // 2)
    return np.concatenate([2 * pair, 2 * pair + 1])


def tables():
    row, lane = np.arange(WORK), np.arange(LANES)
    half = np.arange(WORK // 2)
    order = np.concatenate([2 * half, 2 * half + 1])
    offset = (LANES * order[:, None] + lane[None, :])[None]
    frequency = (np.arange(N_CTX)[None, :] + 32 * np.arange(2)[:, None])[:, :, None, None]
    block = np.stack(phases(offset * frequency, LENGTH), axis=1).astype(np.float32)
    lane_phase = np.stack(phases(row[:, None] * lane[None, :], 4096)).astype(np.float32)

    def parts(matrix):
        high = matrix.astype(ml_dtypes.bfloat16)
        return high, (matrix - high.astype(np.float64)).astype(ml_dtypes.bfloat16)

    cosine, sine = phases(row[:, None] * order[None, :], WORK)
    row_matrices = []
    for matrix in (np.block([[cosine, -sine], [sine, cosine]]), np.block([[cosine.T, sine.T], [-sine.T, cosine.T]])):
        high, low = parts(matrix)
        row_matrices.append(np.concatenate([high, high, low], axis=1))
    order = np.concatenate([np.arange(0, LANES, 2), np.arange(1, LANES, 2)])
    cosine, sine = phases(lane[:, None] * order[None, :], LANES)
    forward = np.block([[cosine, sine], [-sine, cosine]])
    inverse = np.block([[cosine.T, -sine.T], [sine.T, cosine.T]]) / (4 * LENGTH)
    lane_matrices = []
    for matrix in (forward, inverse):
        high, low = parts(matrix)
        lane_matrices.append(np.concatenate([high, high, low], axis=0))
    return block, lane_phase, np.stack(row_matrices), np.stack(lane_matrices)


def call(kernel, out_shape, scratch, *operands, scalars=0):
    return pl.pallas_call(
        kernel,
        out_shape=jax.ShapeDtypeStruct(*out_shape),
        in_specs=[pl.BlockSpec(memory_space=pltpu.SMEM)] * scalars
        + [pl.BlockSpec(memory_space=pltpu.VMEM)] * (len(operands) - scalars),
        out_specs=pl.BlockSpec(memory_space=pltpu.VMEM),
        scratch_shapes=[pltpu.VMEM(shape, F32) for shape in scratch],
        compiler_params=pltpu.CompilerParams(vmem_limit_bytes=VMEM_LIMIT),
    )(*operands)


def apply_filter(core, received):
    block, *others = (jnp.asarray(table) for table in tables())
    block = lax.dynamic_index_in_dim(block, core[0], 0, keepdims=False)
    return call(
        filter_kernel,
        ((N_CTX, ROWS, LANES), BF16),
        [(N_CTX, ROWS, LANES), (2 * WORK, N_CTX * LANES)],
        core,
        received,
        block,
        *others,
        scalars=1,
    )


def exchange(x, axis):
    return lax.all_to_all(x, axis, split_axis=0, concat_axis=0, tiled=True)


def body(value_branch, key_branch, gate_branch, skip_gain, spectra):
    core = (lax.axis_index("ctx") & 1)[None]
    packed = call(pack_kernel, ((N_CHAN, 48, LANES), BF16), [(N_CHAN, 48, LANES)], key_branch, value_branch)
    blocks = call(
        spectra_kernel,
        ((2 * GROUP, ROWS, LANES), BF16),
        [(2 * LANES, ROWS)],
        spectra.reshape(2, GROUP, ROWS, LANES),
    )
    gathered = exchange(packed, "chan")
    sent = call(fan_out_kernel, ((N_CTX, 2 * ROWS, LANES), BF16), [(N_CHAN * 48, LANES)], gathered, blocks)
    received = exchange(sent, "ctx")
    parts = exchange(apply_filter(core, received), "ctx")
    joined = call(join_kernel, ((N_CHAN, 48, LANES), BF16), [(N_CHAN * 48, LANES)], parts)
    tokens = exchange(joined, "chan")
    return call(
        gate_kernel,
        ((CHANNELS, TOKENS), BF16),
        [(N_CHAN, 48, LANES), (CHANNELS, TOKENS)],
        tokens,
        key_branch,
        value_branch,
        gate_branch,
        skip_gain[:, None],
    )


def solution(mesh):
    in_specs = (
        P(None, ("ctx", "chan")),
        P(None, ("ctx", "chan")),
        P(None, ("ctx", "chan")),
        P(),
        P(None, "chan", "ctx", None),
    )
    out_specs = P(None, ("ctx", "chan"))
    return jax.shard_map(body, mesh=mesh, in_specs=in_specs, out_specs=out_specs, check_vma=False)
```

```python
import math

import jax
import jax.numpy as jnp
import ml_dtypes
import numpy as np
from jax import lax
from jax.experimental import pallas as pl
from jax.experimental.pallas import tpu as pltpu
from jax.sharding import PartitionSpec as P

N_CTX = 32
N_CHAN = 16
CHANNELS = 192
GROUP = CHANNELS // N_CHAN
TOKENS = 512
SEQ = 8192
LENGTH = SEQ * N_CTX
LANES = 128
HALF = 16
ROWS = SEQ // LANES
WORK = ROWS // 2
CHIPS = [chip for chip in range(HALF) if (chip + chip // 4) % 4 != 3]
F32 = jnp.float32
BF16 = jnp.bfloat16
VMEM_LIMIT = 32 * 1024 * 1024
WHOLE_VMEM = 64 * 1024 * 1024 - 256 * 1024


def rev5(number):
    return int(f"{number:05b}"[::-1], 2)


def c_root(a, turn, sign):
    if turn == 0:
        return a
    if turn == 0.25:
        return (-a[1], a[0]) if sign > 0 else (a[1], -a[0])
    cosine = math.cos(2 * math.pi * turn)
    sine = sign * math.sin(2 * math.pi * turn)
    return (a[0] * cosine - a[1] * sine, a[0] * sine + a[1] * cosine)


def c_mul(a, re, im):
    return (a[0] * re - a[1] * im, a[0] * im + a[1] * re)


def fft_list(terms, sign):
    size = len(terms)
    if size == 1:
        return terms
    even = fft_list(terms[0::2], sign)
    odd = fft_list(terms[1::2], sign)
    odd = [c_root(term, index / size, sign) for index, term in enumerate(odd)]
    return [(e[0] + o[0], e[1] + o[1]) for e, o in zip(even, odd)] + [
        (e[0] - o[0], e[1] - o[1]) for e, o in zip(even, odd)
    ]


def start(copy):
    copy.start()
    return copy


def pack_kernel(key_far, value_far, out_far, key_ref, value_ref, wide, out_ref, arrived, left):
    low = lax.broadcasted_iota(jnp.int32, (8, LANES), 0) < 4
    fetches, sends = [], []
    for half in range(2):
        rows = pl.ds(half * CHANNELS // 2, CHANNELS // 2)
        for index, (far, near) in enumerate(((key_far, key_ref), (value_far, value_ref))):
            fetches.append(start(pltpu.make_async_copy(far.at[rows], near.at[rows], arrived.at[half, index])))
    for block in range(CHANNELS // 16):
        if block % 6 == 0:
            fetches[block // 3].wait()
            fetches[block // 3 + 1].wait()
        rows = slice(16 * block, 16 * block + 16)
        carried = (key_ref[rows, :].astype(F32) * value_ref[rows, :].astype(F32)).astype(BF16).astype(F32)
        for part in range(2):
            for upper in range(2):
                a = carried[8 * part : 8 * part + 8, 256 * upper : 256 * upper + 128]
                b = carried[8 * part : 8 * part + 8, 256 * upper + 128 : 256 * upper + 256]
                first = jnp.where(low, a, pltpu.roll(b, 4, 0))
                second = jnp.where(low, pltpu.roll(a, 4, 0), b)
                for offset, piece in enumerate((first, second)):
                    quad = 4 * block + 2 * part + offset
                    row = 24 * upper + 8 * (quad % 3)
                    wide[quad // 3, row : row + 8, :] = piece
        if block % 6 == 5:
            first = N_CHAN // 2 * (block // 6)
            for target in range(first, first + N_CHAN // 2):
                out_ref[target] = wide[target].astype(BF16)
            targets = pl.ds(first, N_CHAN // 2)
            sends.append(start(pltpu.make_async_copy(out_ref.at[targets], out_far.at[targets], left.at[block // 6])))
    for send in sends:
        send.wait()


def gate_kernel(conv_ref, key_ref, value_ref, gate_ref, skip_ref, out_far, wide, flat, out_ref, left):
    low = lax.broadcasted_iota(jnp.int32, (8, LANES), 0) < 4
    sends = []
    for block in range(CHANNELS // 8):
        for upper in range(2):
            pieces = []
            for offset in range(2):
                quad = 2 * block + offset
                row = 24 * upper + 8 * (quad % 3)
                if row == 0:
                    wide[quad // 3] = conv_ref[quad // 3].astype(F32)
                pieces.append(wide[quad // 3, row : row + 8, :])
            first, second = pieces
            flat[8 * block : 8 * block + 8, 256 * upper : 256 * upper + 128] = jnp.where(
                low, first, pltpu.roll(second, 4, 0)
            )
            flat[8 * block : 8 * block + 8, 256 * upper + 128 : 256 * upper + 256] = jnp.where(
                low, pltpu.roll(first, 4, 0), second
            )
        if block % 2 == 1:
            rows = slice(8 * block - 8, 8 * block + 8)
            carried = (key_ref[rows, :].astype(F32) * value_ref[rows, :].astype(F32)).astype(BF16).astype(F32)
            total = flat[rows, :] + skip_ref[rows, :] * carried
            out_ref[rows, :] = (gate_ref[rows, :].astype(F32) * total).astype(BF16)
        if block % 6 == 5:
            rows = pl.ds(8 * block - 40, 48)
            sends.append(start(pltpu.make_async_copy(out_ref.at[rows], out_far.at[rows], left.at[block // 6])))
    for send in sends:
        send.wait()


def fan_out_kernel(in_ref, blocks_ref, out_far, wide, out_ref, left):
    for source in range(N_CHAN):
        wide[48 * source : 48 * source + 48, :] = in_ref[source].astype(F32)
    sends = []
    for chip in range(HALF):
        if chip in CHIPS:
            channel = CHIPS.index(chip)
            first = 8 * (channel // 4) + channel % 4
            pieces = [wide[pl.ds(first + 4 * quarter, ROWS // 2, stride=24), :] for quarter in range(2)]
            series = jnp.concatenate(pieces, axis=0).astype(BF16)
            for core in range(2):
                out_ref[2 * chip + core, 0:ROWS, :] = series
                out_ref[2 * chip + core, ROWS : 2 * ROWS, :] = blocks_ref[2 * channel + core]
        else:
            for core in range(2):
                out_ref[2 * chip + core] = jnp.zeros((2 * ROWS, LANES), BF16)
        if chip % 4 == 3:
            targets = pl.ds(2 * chip - 6, 8)
            sends.append(start(pltpu.make_async_copy(out_ref.at[targets], out_far.at[targets], left.at[chip // 4])))
    for send in sends:
        send.wait()


def join_kernel(in_ref, out_ref, wide):
    for channel, chip in enumerate(CHIPS):
        total = in_ref[2 * chip].astype(F32) + in_ref[2 * chip + 1].astype(F32)
        first = 8 * (channel // 4) + channel % 4
        for quarter in range(2):
            wide[pl.ds(first + 4 * quarter, ROWS // 2, stride=24), :] = total[
                ROWS // 2 * quarter : ROWS // 2 * quarter + ROWS // 2
            ]
    for target in range(N_CHAN):
        out_ref[target] = wide[48 * target : 48 * target + 48, :].astype(BF16)


def spectra_kernel(in_ref, out_ref, turned):
    for channel in range(GROUP):
        for part in range(2):
            turned[LANES * part : LANES * part + LANES, :] = in_ref[part, channel].T
        for core in range(2):
            parts = []
            for part in range(2):
                starts = [LANES * part + 64 * upper + core for upper in range(2)]
                halves = [turned[pl.ds(start, 32, stride=2), :] for start in starts]
                parts.append(jnp.concatenate(halves, axis=1))
            out_ref[2 * channel + core] = jnp.concatenate(parts, axis=0).astype(BF16)


def split(x):
    high = x.astype(BF16)
    return high, (x - high.astype(F32)).astype(BF16)


def dot(a, b):
    return jnp.dot(a, b, preferred_element_type=F32)


def filter_kernel(core_ref, in_ref, block_ref, row_matrix_ref, lane_matrix_ref, out_ref, real, pair):
    sign = jnp.where(core_ref[0] == 0, 1.0, -1.0).astype(F32)
    for index in range(N_CTX):
        real[index] = in_ref[index, 0:ROWS, :].astype(F32)

    def places(group):
        start = 32 * (group // 2) + 8 * (group % 2)
        return slice(start, start + 8), slice(start + 16, start + 24), 8 * group

    for group in range(WORK // 8):
        early, late, row = places(group)
        sums = fft_list([(real[p, early, :], sign * real[p, late, :]) for p in range(N_CTX)], -1)
        for residue in range(N_CTX):
            here, mirror = sums[residue], sums[-residue % N_CTX]
            first = (here[0] + mirror[0], here[1] - mirror[1])
            second = (here[1] + mirror[1], mirror[0] - here[0])
            second = c_root(second, residue / 64, -1)
            term = (first[0] + second[0], first[1] + second[1])
            rows = slice(row, row + 8)
            term = c_mul(term, block_ref[0, residue, rows, :], block_ref[1, residue, rows, :])
            columns = slice(LANES * residue, LANES * residue + LANES)
            pair[row : row + 8, columns] = term[0]
            pair[WORK + row : WORK + row + 8, columns] = term[1]
    lane_re, lane_im = block_ref[0, N_CTX], block_ref[1, N_CTX]
    high, low = split(pair[...])
    mixed = dot(row_matrix_ref[0], jnp.concatenate([high, low, high], axis=0))
    turned = []
    for index in range(N_CTX):
        lanes = slice(LANES * index, LANES * index + LANES)
        term = c_mul((mixed[:WORK, lanes], mixed[WORK:, lanes]), lane_re, lane_im)
        turned.append(jnp.concatenate(term, axis=1))
    high, low = split(jnp.concatenate(turned, axis=0))
    spectrum = dot(jnp.concatenate([high, low, high], axis=1), lane_matrix_ref[0])
    shaped = []
    for index in range(N_CTX):
        rows = slice(WORK * index, WORK * index + WORK)
        response = in_ref[rev5(index), ROWS : 2 * ROWS, :].astype(F32)
        term = c_mul((spectrum[rows, :LANES], spectrum[rows, LANES:]), response[:WORK], response[WORK:])
        shaped.append(jnp.concatenate(term, axis=1))
    high, low = split(jnp.concatenate(shaped, axis=0))
    mixed = dot(jnp.concatenate([high, low, high], axis=1), lane_matrix_ref[1])
    turned = []
    for index in range(N_CTX):
        rows = slice(WORK * index, WORK * index + WORK)
        term = c_mul((mixed[rows, :LANES], mixed[rows, LANES:]), lane_re, -lane_im)
        turned.append(jnp.concatenate(term, axis=0))
    high, low = split(jnp.concatenate(turned, axis=1))
    pair[...] = dot(row_matrix_ref[1], jnp.concatenate([high, low, high], axis=0))
    for group in range(WORK // 8):
        early, late, row = places(group)
        rows = slice(row, row + 8)
        evens, odds = [], []
        for residue in range(N_CTX):
            columns = slice(LANES * residue, LANES * residue + LANES)
            term = (pair[row : row + 8, columns], pair[WORK + row : WORK + row + 8, columns])
            term = c_mul(term, block_ref[0, residue, rows, :], -block_ref[1, residue, rows, :])
            evens.append(term)
            odds.append(c_root(term, residue / 64, 1))
        terms = []
        for residue in range(N_CTX):
            mirror = -residue % N_CTX
            even = (evens[residue][0] + evens[mirror][0], evens[residue][1] - evens[mirror][1])
            odd = (odds[residue][0] + odds[mirror][0], odds[residue][1] - odds[mirror][1])
            terms.append((even[0] - odd[1], even[1] + odd[0]))
        for p, term in enumerate(fft_list(terms, 1)):
            real[p, early, :] = term[0]
            real[p, late, :] = sign * term[1]
    for index in range(N_CTX):
        out_ref[index] = real[index].astype(BF16)


def phases(numerator, denominator):
    angle = -2 * np.pi * (numerator % denominator) / denominator
    return np.cos(angle), np.sin(angle)


def row_order():
    pair = np.arange(ROWS // 2)
    return np.concatenate([2 * pair, 2 * pair + 1])


def tables():
    row, lane = np.arange(WORK), np.arange(LANES)
    half = np.arange(WORK // 2)
    order = np.concatenate([2 * half, 2 * half + 1])
    offset = (LANES * order[:, None] + lane[None, :])[None]
    frequency = (np.arange(N_CTX)[None, :] + 32 * np.arange(2)[:, None])[:, :, None, None]
    block = np.stack(phases(offset * frequency, LENGTH), axis=1).astype(np.float32)
    lane_phase = np.stack(phases(row[:, None] * lane[None, :], 4096)).astype(np.float32)
    block = np.concatenate([block, np.stack([lane_phase] * 2)[:, :, None]], axis=2)

    def parts(matrix):
        high = matrix.astype(ml_dtypes.bfloat16)
        return high, (matrix - high.astype(np.float64)).astype(ml_dtypes.bfloat16)

    cosine, sine = phases(row[:, None] * order[None, :], WORK)
    row_matrices = []
    for matrix in (np.block([[cosine, -sine], [sine, cosine]]), np.block([[cosine.T, sine.T], [-sine.T, cosine.T]])):
        high, low = parts(matrix)
        row_matrices.append(np.concatenate([high, high, low], axis=1))
    order = np.concatenate([np.arange(0, LANES, 2), np.arange(1, LANES, 2)])
    cosine, sine = phases(lane[:, None] * order[None, :], LANES)
    forward = np.block([[cosine, sine], [-sine, cosine]])
    inverse = np.block([[cosine.T, -sine.T], [sine.T, cosine.T]]) / (4 * LENGTH)
    lane_matrices = []
    for matrix in (forward, inverse):
        high, low = parts(matrix)
        lane_matrices.append(np.concatenate([high, high, low], axis=0))
    return block, np.stack(row_matrices), np.stack(lane_matrices)


def call(kernel, out_shape, scratch, *operands, scalars=0, far_in=False, far_out=False, limit=VMEM_LIMIT):
    near_in = pltpu.HBM if far_in else pltpu.VMEM
    return pl.pallas_call(
        kernel,
        out_shape=jax.ShapeDtypeStruct(*out_shape),
        in_specs=[pl.BlockSpec(memory_space=pltpu.SMEM)] * scalars
        + [pl.BlockSpec(memory_space=near_in)] * (len(operands) - scalars),
        out_specs=pl.BlockSpec(memory_space=pltpu.HBM if far_out else pltpu.VMEM),
        scratch_shapes=[pltpu.VMEM(shape, F32) if isinstance(shape, tuple) else shape for shape in scratch],
        compiler_params=pltpu.CompilerParams(vmem_limit_bytes=limit),
    )(*operands)


def apply_filter(core, received):
    block, *others = (jnp.asarray(table) for table in tables())
    block = lax.dynamic_index_in_dim(block, core[0], 0, keepdims=False)
    return call(
        filter_kernel,
        ((N_CTX, ROWS, LANES), BF16),
        [(N_CTX, ROWS, LANES), (2 * WORK, N_CTX * LANES)],
        core,
        received,
        block,
        *others,
        scalars=1,
    )


def exchange(x, axis):
    return lax.all_to_all(x, axis, split_axis=0, concat_axis=0, tiled=True)


def body(value_branch, key_branch, gate_branch, skip_gain, spectra):
    core = (lax.axis_index("ctx") & 1)[None]
    tokens_shape, message = (CHANNELS, TOKENS), (N_CHAN, 48, LANES)
    semaphores = pltpu.SemaphoreType.DMA
    packed = call(
        pack_kernel,
        (message, BF16),
        [
            pltpu.VMEM(tokens_shape, BF16),
            pltpu.VMEM(tokens_shape, BF16),
            message,
            pltpu.VMEM(message, BF16),
            semaphores((2, 2)),
            semaphores((2,)),
        ],
        key_branch,
        value_branch,
        far_in=True,
        far_out=True,
        limit=WHOLE_VMEM,
    )
    blocks = call(
        spectra_kernel,
        ((2 * GROUP, ROWS, LANES), BF16),
        [(2 * LANES, ROWS)],
        spectra.reshape(2, GROUP, ROWS, LANES),
    )
    gathered = exchange(packed, "chan")
    blocks_shape = (N_CTX, 2 * ROWS, LANES)
    sent = call(
        fan_out_kernel,
        (blocks_shape, BF16),
        [(N_CHAN * 48, LANES), pltpu.VMEM(blocks_shape, BF16), semaphores((4,))],
        gathered,
        blocks,
        far_out=True,
    )
    received = exchange(sent, "ctx")
    parts = exchange(apply_filter(core, received), "ctx")
    joined = call(join_kernel, ((N_CHAN, 48, LANES), BF16), [(N_CHAN * 48, LANES)], parts)
    tokens = exchange(joined, "chan")
    return call(
        gate_kernel,
        (tokens_shape, BF16),
        [message, tokens_shape, pltpu.VMEM(tokens_shape, BF16), semaphores((4,))],
        tokens,
        key_branch,
        value_branch,
        gate_branch,
        skip_gain[:, None],
        far_out=True,
    )


def solution(mesh):
    in_specs = (
        P(None, ("ctx", "chan")),
        P(None, ("ctx", "chan")),
        P(None, ("ctx", "chan")),
        P(),
        P(None, "chan", "ctx", None),
    )
    out_specs = P(None, ("ctx", "chan"))
    return jax.shard_map(body, mesh=mesh, in_specs=in_specs, out_specs=out_specs, check_vma=False)
```

```python
import math

import jax
import jax.numpy as jnp
import ml_dtypes
import numpy as np
from jax import lax
from jax.experimental import pallas as pl
from jax.experimental.pallas import tpu as pltpu
from jax.sharding import PartitionSpec as P

N_CTX = 32
N_CHAN = 16
CHANNELS = 192
GROUP = CHANNELS // N_CHAN
TOKENS = 512
SEQ = 8192
LENGTH = SEQ * N_CTX
LANES = 128
HALF = 16
ROWS = SEQ // LANES
WORK = ROWS // 2
CHIPS = [chip for chip in range(HALF) if (chip + chip // 4) % 4 != 3]
F32 = jnp.float32
BF16 = jnp.bfloat16
VMEM_LIMIT = 32 * 1024 * 1024
WHOLE_VMEM = 64 * 1024 * 1024 - 256 * 1024


def rev5(number):
    return int(f"{number:05b}"[::-1], 2)


def c_root(a, turn, sign):
    if turn == 0:
        return a
    if turn == 0.25:
        return (-a[1], a[0]) if sign > 0 else (a[1], -a[0])
    cosine = math.cos(2 * math.pi * turn)
    sine = sign * math.sin(2 * math.pi * turn)
    return (a[0] * cosine - a[1] * sine, a[0] * sine + a[1] * cosine)


def c_mul(a, re, im):
    return (a[0] * re - a[1] * im, a[0] * im + a[1] * re)


def fft_list(terms, sign):
    size = len(terms)
    if size == 1:
        return terms
    even = fft_list(terms[0::2], sign)
    odd = fft_list(terms[1::2], sign)
    odd = [c_root(term, index / size, sign) for index, term in enumerate(odd)]
    return [(e[0] + o[0], e[1] + o[1]) for e, o in zip(even, odd)] + [
        (e[0] - o[0], e[1] - o[1]) for e, o in zip(even, odd)
    ]


def start(copy):
    copy.start()
    return copy


def pack_kernel(key_far, value_far, out_far, key_ref, value_ref, wide, out_ref, arrived, left):
    low = lax.broadcasted_iota(jnp.int32, (8, LANES), 0) < 4
    fetches, sends = [], []
    for half in range(2):
        rows = pl.ds(half * CHANNELS // 2, CHANNELS // 2)
        for index, (far, near) in enumerate(((key_far, key_ref), (value_far, value_ref))):
            fetches.append(start(pltpu.make_async_copy(far.at[rows], near.at[rows], arrived.at[half, index])))
    for block in range(CHANNELS // 16):
        if block % 6 == 0:
            fetches[block // 3].wait()
            fetches[block // 3 + 1].wait()
        rows = slice(16 * block, 16 * block + 16)
        carried = (key_ref[rows, :].astype(F32) * value_ref[rows, :].astype(F32)).astype(BF16).astype(F32)
        for part in range(2):
            for upper in range(2):
                a = carried[8 * part : 8 * part + 8, 256 * upper : 256 * upper + 128]
                b = carried[8 * part : 8 * part + 8, 256 * upper + 128 : 256 * upper + 256]
                first = jnp.where(low, a, pltpu.roll(b, 4, 0))
                second = jnp.where(low, pltpu.roll(a, 4, 0), b)
                for offset, piece in enumerate((first, second)):
                    quad = 4 * block + 2 * part + offset
                    row = 24 * upper + 8 * (quad % 3)
                    wide[quad // 3, row : row + 8, :] = piece
        if block % 6 == 5:
            first = N_CHAN // 2 * (block // 6)
            for target in range(first, first + N_CHAN // 2):
                out_ref[target] = wide[target].astype(BF16)
            targets = pl.ds(first, N_CHAN // 2)
            sends.append(start(pltpu.make_async_copy(out_ref.at[targets], out_far.at[targets], left.at[block // 6])))
    for send in sends:
        send.wait()


def gate_kernel(conv_ref, key_ref, value_ref, gate_ref, skip_ref, out_far, wide, flat, out_ref, left):
    low = lax.broadcasted_iota(jnp.int32, (8, LANES), 0) < 4
    sends = []
    for block in range(CHANNELS // 8):
        for upper in range(2):
            pieces = []
            for offset in range(2):
                quad = 2 * block + offset
                row = 24 * upper + 8 * (quad % 3)
                if row == 0:
                    wide[quad // 3] = conv_ref[quad // 3].astype(F32)
                pieces.append(wide[quad // 3, row : row + 8, :])
            first, second = pieces
            flat[8 * block : 8 * block + 8, 256 * upper : 256 * upper + 128] = jnp.where(
                low, first, pltpu.roll(second, 4, 0)
            )
            flat[8 * block : 8 * block + 8, 256 * upper + 128 : 256 * upper + 256] = jnp.where(
                low, pltpu.roll(first, 4, 0), second
            )
        if block % 2 == 1:
            rows = slice(8 * block - 8, 8 * block + 8)
            carried = (key_ref[rows, :].astype(F32) * value_ref[rows, :].astype(F32)).astype(BF16).astype(F32)
            total = flat[rows, :] + skip_ref[rows, :] * carried
            out_ref[rows, :] = (gate_ref[rows, :].astype(F32) * total).astype(BF16)
        if block % 6 == 5:
            rows = pl.ds(8 * block - 40, 48)
            sends.append(start(pltpu.make_async_copy(out_ref.at[rows], out_far.at[rows], left.at[block // 6])))
    for send in sends:
        send.wait()


def fan_out_kernel(in_ref, blocks_ref, out_far, wide, out_ref, left):
    for source in range(N_CHAN):
        wide[48 * source : 48 * source + 48, :] = in_ref[source].astype(F32)
    sends = []
    for chip in range(HALF):
        if chip in CHIPS:
            channel = CHIPS.index(chip)
            first = 8 * (channel // 4) + channel % 4
            pieces = [wide[pl.ds(first + 4 * quarter, ROWS // 2, stride=24), :] for quarter in range(2)]
            series = jnp.concatenate(pieces, axis=0).astype(BF16)
            for core in range(2):
                out_ref[2 * chip + core, 0:ROWS, :] = series
                out_ref[2 * chip + core, ROWS : 2 * ROWS, :] = blocks_ref[2 * channel + core]
        else:
            for core in range(2):
                out_ref[2 * chip + core] = jnp.zeros((2 * ROWS, LANES), BF16)
        if chip % 4 == 3:
            targets = pl.ds(2 * chip - 6, 8)
            sends.append(start(pltpu.make_async_copy(out_ref.at[targets], out_far.at[targets], left.at[chip // 4])))
    for send in sends:
        send.wait()


def join_kernel(in_ref, out_ref, wide):
    for channel, chip in enumerate(CHIPS):
        total = in_ref[2 * chip].astype(F32) + in_ref[2 * chip + 1].astype(F32)
        first = 8 * (channel // 4) + channel % 4
        for quarter in range(2):
            wide[pl.ds(first + 4 * quarter, ROWS // 2, stride=24), :] = total[
                ROWS // 2 * quarter : ROWS // 2 * quarter + ROWS // 2
            ]
    for target in range(N_CHAN):
        out_ref[target] = wide[48 * target : 48 * target + 48, :].astype(BF16)


def spectra_kernel(in_ref, out_ref, turned):
    for channel in range(GROUP):
        for part in range(2):
            turned[LANES * part : LANES * part + LANES, :] = in_ref[part, channel].T
        for core in range(2):
            parts = []
            for part in range(2):
                starts = [LANES * part + 64 * upper + core for upper in range(2)]
                halves = [turned[pl.ds(start, 32, stride=2), :] for start in starts]
                parts.append(jnp.concatenate(halves, axis=1))
            out_ref[2 * channel + core] = jnp.concatenate(parts, axis=0).astype(BF16)


def split(x):
    high = x.astype(BF16)
    return high, (x - high.astype(F32)).astype(BF16)


def dot(a, b):
    return jnp.dot(a, b, preferred_element_type=F32)


def filter_kernel(core_ref, in_ref, block_ref, matrix_ref, out_ref, real, pair):
    sign = jnp.where(core_ref[0] == 0, 1.0, -1.0).astype(F32)
    for index in range(N_CTX):
        real[index] = in_ref[index, 0:ROWS, :].astype(F32)

    def places(group):
        start = 32 * (group // 2) + 8 * (group % 2)
        return slice(start, start + 8), slice(start + 16, start + 24), 8 * group

    for group in range(WORK // 8):
        early, late, row = places(group)
        sums = fft_list([(real[p, early, :], sign * real[p, late, :]) for p in range(N_CTX)], -1)
        for residue in range(N_CTX):
            here, mirror = sums[residue], sums[-residue % N_CTX]
            first = (here[0] + mirror[0], here[1] - mirror[1])
            second = (here[1] + mirror[1], mirror[0] - here[0])
            second = c_root(second, residue / 64, -1)
            term = (first[0] + second[0], first[1] + second[1])
            rows = slice(row, row + 8)
            term = c_mul(term, block_ref[0, residue, rows, :], block_ref[1, residue, rows, :])
            columns = slice(LANES * residue, LANES * residue + LANES)
            pair[row : row + 8, columns] = term[0]
            pair[WORK + row : WORK + row + 8, columns] = term[1]
    lane_re, lane_im = block_ref[0, N_CTX], block_ref[1, N_CTX]
    high, low = split(pair[...])
    mixed = dot(matrix_ref[0, 6 * LANES :, : 3 * ROWS], jnp.concatenate([high, low, high], axis=0))
    turned = []
    for index in range(N_CTX):
        lanes = slice(LANES * index, LANES * index + LANES)
        term = c_mul((mixed[:WORK, lanes], mixed[WORK:, lanes]), lane_re, lane_im)
        turned.append(jnp.concatenate(term, axis=1))
    high, low = split(jnp.concatenate(turned, axis=0))
    spectrum = dot(jnp.concatenate([high, low, high], axis=1), matrix_ref[0, : 6 * LANES, :])
    shaped = []
    for index in range(N_CTX):
        rows = slice(WORK * index, WORK * index + WORK)
        response = in_ref[rev5(index), ROWS : 2 * ROWS, :].astype(F32)
        term = c_mul((spectrum[rows, :LANES], spectrum[rows, LANES:]), response[:WORK], response[WORK:])
        shaped.append(jnp.concatenate(term, axis=1))
    high, low = split(jnp.concatenate(shaped, axis=0))
    mixed = dot(jnp.concatenate([high, low, high], axis=1), matrix_ref[1, : 6 * LANES, :])
    turned = []
    for index in range(N_CTX):
        rows = slice(WORK * index, WORK * index + WORK)
        term = c_mul((mixed[rows, :LANES], mixed[rows, LANES:]), lane_re, -lane_im)
        turned.append(jnp.concatenate(term, axis=0))
    high, low = split(jnp.concatenate(turned, axis=1))
    pair[...] = dot(matrix_ref[1, 6 * LANES :, : 3 * ROWS], jnp.concatenate([high, low, high], axis=0))
    for group in range(WORK // 8):
        early, late, row = places(group)
        rows = slice(row, row + 8)
        evens, odds = [], []
        for residue in range(N_CTX):
            columns = slice(LANES * residue, LANES * residue + LANES)
            term = (pair[row : row + 8, columns], pair[WORK + row : WORK + row + 8, columns])
            term = c_mul(term, block_ref[0, residue, rows, :], -block_ref[1, residue, rows, :])
            evens.append(term)
            odds.append(c_root(term, residue / 64, 1))
        terms = []
        for residue in range(N_CTX):
            mirror = -residue % N_CTX
            even = (evens[residue][0] + evens[mirror][0], evens[residue][1] - evens[mirror][1])
            odd = (odds[residue][0] + odds[mirror][0], odds[residue][1] - odds[mirror][1])
            terms.append((even[0] - odd[1], even[1] + odd[0]))
        for p, term in enumerate(fft_list(terms, 1)):
            real[p, early, :] = term[0]
            real[p, late, :] = sign * term[1]
    for index in range(N_CTX):
        out_ref[index] = real[index].astype(BF16)


def phases(numerator, denominator):
    angle = -2 * np.pi * (numerator % denominator) / denominator
    return np.cos(angle), np.sin(angle)


def row_order():
    pair = np.arange(ROWS // 2)
    return np.concatenate([2 * pair, 2 * pair + 1])


def tables():
    row, lane = np.arange(WORK), np.arange(LANES)
    half = np.arange(WORK // 2)
    order = np.concatenate([2 * half, 2 * half + 1])
    offset = (LANES * order[:, None] + lane[None, :])[None]
    frequency = (np.arange(N_CTX)[None, :] + 32 * np.arange(2)[:, None])[:, :, None, None]
    block = np.stack(phases(offset * frequency, LENGTH), axis=1).astype(np.float32)
    lane_phase = np.stack(phases(row[:, None] * lane[None, :], 4096)).astype(np.float32)
    block = np.concatenate([block, np.stack([lane_phase] * 2)[:, :, None]], axis=2)

    def parts(matrix):
        high = matrix.astype(ml_dtypes.bfloat16)
        return high, (matrix - high.astype(np.float64)).astype(ml_dtypes.bfloat16)

    cosine, sine = phases(row[:, None] * order[None, :], WORK)
    row_matrices = []
    for matrix in (np.block([[cosine, -sine], [sine, cosine]]), np.block([[cosine.T, sine.T], [-sine.T, cosine.T]])):
        high, low = parts(matrix)
        row_matrices.append(np.concatenate([high, high, low], axis=1))
    order = np.concatenate([np.arange(0, LANES, 2), np.arange(1, LANES, 2)])
    cosine, sine = phases(lane[:, None] * order[None, :], LANES)
    forward = np.block([[cosine, sine], [-sine, cosine]])
    inverse = np.block([[cosine.T, -sine.T], [sine.T, cosine.T]]) / (4 * LENGTH)
    lane_matrices = []
    for matrix in (forward, inverse):
        high, low = parts(matrix)
        lane_matrices.append(np.concatenate([high, high, low], axis=0))
    matrices = np.zeros((2, 6 * LANES + ROWS, 2 * LANES), ml_dtypes.bfloat16)
    matrices[:, : 6 * LANES] = np.stack(lane_matrices)
    matrices[:, 6 * LANES :, : 3 * ROWS] = np.stack(row_matrices)
    return block, matrices


def call(kernel, out_shape, scratch, *operands, scalars=0, far_in=False, far_out=False, limit=VMEM_LIMIT):
    near_in = pltpu.HBM if far_in else pltpu.VMEM
    return pl.pallas_call(
        kernel,
        out_shape=jax.ShapeDtypeStruct(*out_shape),
        in_specs=[pl.BlockSpec(memory_space=pltpu.SMEM)] * scalars
        + [pl.BlockSpec(memory_space=near_in)] * (len(operands) - scalars),
        out_specs=pl.BlockSpec(memory_space=pltpu.HBM if far_out else pltpu.VMEM),
        scratch_shapes=[pltpu.VMEM(shape, F32) if isinstance(shape, tuple) else shape for shape in scratch],
        compiler_params=pltpu.CompilerParams(vmem_limit_bytes=limit),
    )(*operands)


def apply_filter(core, received):
    block, matrices = (jnp.asarray(table) for table in tables())
    block = lax.dynamic_index_in_dim(block, core[0], 0, keepdims=False)
    return call(
        filter_kernel,
        ((N_CTX, ROWS, LANES), BF16),
        [(N_CTX, ROWS, LANES), (2 * WORK, N_CTX * LANES)],
        core,
        received,
        block,
        matrices,
        scalars=1,
    )


def exchange(x, axis):
    return lax.all_to_all(x, axis, split_axis=0, concat_axis=0, tiled=True)


def body(value_branch, key_branch, gate_branch, skip_gain, spectra):
    core = (lax.axis_index("ctx") & 1)[None]
    tokens_shape, message = (CHANNELS, TOKENS), (N_CHAN, 48, LANES)
    semaphores = pltpu.SemaphoreType.DMA
    packed = call(
        pack_kernel,
        (message, BF16),
        [
            pltpu.VMEM(tokens_shape, BF16),
            pltpu.VMEM(tokens_shape, BF16),
            message,
            pltpu.VMEM(message, BF16),
            semaphores((2, 2)),
            semaphores((2,)),
        ],
        key_branch,
        value_branch,
        far_in=True,
        far_out=True,
        limit=WHOLE_VMEM,
    )
    blocks = call(
        spectra_kernel,
        ((2 * GROUP, ROWS, LANES), BF16),
        [(2 * LANES, ROWS)],
        spectra.reshape(2, GROUP, ROWS, LANES),
    )
    gathered = exchange(packed, "chan")
    blocks_shape = (N_CTX, 2 * ROWS, LANES)
    sent = call(
        fan_out_kernel,
        (blocks_shape, BF16),
        [(N_CHAN * 48, LANES), pltpu.VMEM(blocks_shape, BF16), semaphores((4,))],
        gathered,
        blocks,
        far_out=True,
    )
    received = exchange(sent, "ctx")
    parts = exchange(apply_filter(core, received), "ctx")
    joined = call(join_kernel, ((N_CHAN, 48, LANES), BF16), [(N_CHAN * 48, LANES)], parts)
    tokens = exchange(joined, "chan")
    return call(
        gate_kernel,
        (tokens_shape, BF16),
        [message, tokens_shape, pltpu.VMEM(tokens_shape, BF16), semaphores((4,))],
        tokens,
        key_branch,
        value_branch,
        gate_branch,
        skip_gain[:, None],
        far_out=True,
    )


def solution(mesh):
    in_specs = (
        P(None, ("ctx", "chan")),
        P(None, ("ctx", "chan")),
        P(None, ("ctx", "chan")),
        P(),
        P(None, "chan", "ctx", None),
    )
    out_specs = P(None, ("ctx", "chan"))
    return jax.shard_map(body, mesh=mesh, in_specs=in_specs, out_specs=out_specs, check_vma=False)
```
